32 devices in a mesh: gx: 4 (over y, x), gy: 8 (over z, core).
Axes of the slice: x: 2, y: 2, z: 4, core: 2. Of those that a mesh axis runs over, the one named last changes fastest.
Arguments:
- starting_sag: float32 [512, 1024], P('gx', 'gy'), may hold values from -6 to 6
- warmth_celsius_field: float32 [512, 1024], P('gx', 'gy'), may hold values from 25 to 125
- junction_charge_store: float32 [512, 1024], P('gx', 'gy'), may hold values from 5e-05 to 0.0005
- load_amperes: float32 [2, 512, 1024], P(None, 'gx', 'gy'), may hold values from -0.08 to 0.08
- source_patch_bits: int32 [16, 32], P('gx', 'gy'), may hold values 0 or 1
Outputs:
- drop: float32 [512, 1024], P('gx', 'gy')
The draws below stay inside these ranges and needn't reach their ends.
All inputs are finite; a program needn't handle non-finite values. No bound on the sum of `source_patch_bits` on one device may be relied on, other than what follows from the above.
Results may differ from the reference program's by a relative error of at most 0.0013.
Values sent between devices are 32-bit elements; how exact they have to be, the bound alone decides.
A program may use at most 64 MiB of HBM per device.

```python
import math
import jax
import jax.numpy as jnp
from jax import lax

STEPS = 2
PITCH = 32
POINTS_EACH_RUN = 512
STRIP_TRACKS = 1024


def draw_load_amperes(key, part):
    rough_key = jax.random.fold_in(key, 0)
    rough_part = jnp.clip(jax.random.normal(rough_key, (STEPS, POINTS_EACH_RUN, STRIP_TRACKS), jnp.float32), -6.0, 6.0) * 0.01
    return rough_part


def place_ends(values, stream_key, smallest, high):
    place = [jax.random.randint(jax.random.fold_in(stream_key, axis), (), 0, length) for axis, length in enumerate(values.shape)]
    longest = values.shape.index(max(values.shape))
    beside = place[:longest] + [(place[longest] + 1) % values.shape[longest]] + place[longest + 1:]
    return values.at[tuple(place)].set(smallest).at[tuple(beside)].set(high)


def block_levels(key, shape, cuts, low, top_value):
    level, own = 1.0, jax.random.fold_in(key, 6)
    for dim, shards_of in cuts:
        steps = jnp.exp(jax.random.uniform(jax.random.fold_in(own, dim), (shards_of,), jnp.float32, low / len(cuts), top_value / len(cuts)))
        level = level * jnp.repeat(steps, shape[dim] // shards_of).reshape([-1 if axis == dim else 1 for axis in range(len(shape))])
    return level


def noise(own_key, shape, spread, bound, cuts=(), kind=jnp.bfloat16):
    entries = jax.random.normal(own_key, shape, jnp.float32) * spread
    if len(cuts) > 0:
        entries = block_levels(own_key, shape, cuts, -0.22, 0.18) * entries
    return jnp.clip(entries, min=-bound, max=bound).astype(kind)


def setup_inputs(seed: int = 0) -> dict:
    arg_keys = jax.random.split(jax.random.key(seed), 6)
    starting_sag = noise(arg_keys[0], (POINTS_EACH_RUN, STRIP_TRACKS), 1.0, 6.0, ((0, 4), (1, 8)), jnp.float32)
    warmth_celsius_field = jnp.clip(25.0 + 100.0 * jax.random.uniform(arg_keys[1], (POINTS_EACH_RUN, STRIP_TRACKS), jnp.float32) ** block_levels(arg_keys[1], (POINTS_EACH_RUN, STRIP_TRACKS), ((0, 4), (1, 8)), -0.2, 0.2), 25.0, 125.0)
    junction_charge_store = jnp.clip(jnp.exp(math.log(0.0005) - 2.3025852 * jax.random.uniform(arg_keys[2], (POINTS_EACH_RUN, STRIP_TRACKS), jnp.float32) ** block_levels(arg_keys[2], (POINTS_EACH_RUN, STRIP_TRACKS), ((0, 4), (1, 8)), -0.2, 0.2)), 4.999999873689376e-05, 0.0005)
    load_amperes = draw_load_amperes(jax.random.fold_in(arg_keys[5], 71), 0)
    source_patch_bits = place_ends((jax.random.randint(arg_keys[4], (POINTS_EACH_RUN // PITCH, STRIP_TRACKS // PITCH), 0, 2) < 1).astype(jnp.int32), jax.random.fold_in(arg_keys[4], 1), 0, 1)
    return dict(starting_sag=starting_sag, warmth_celsius_field=warmth_celsius_field, junction_charge_store=junction_charge_store, load_amperes=load_amperes, source_patch_bits=source_patch_bits)


xward_admittance = 1.0
yward_admittance = 0.5
warmth_scaling = 0.004
surrounding_warmth = 25.0
cushion_pieces = 1.0


def factor(sub_diag, main_diag, sup_diag):
    def advance(prev_ratio, packed):
        sub_row, main_row, sup_row = packed
        pivot_row = 1.0 / (main_row - sub_row * prev_ratio)
        next_ratio = sup_row * pivot_row
        return next_ratio, (pivot_row, next_ratio)

    _, (pivots, ratios) = lax.scan(advance, jnp.zeros_like(main_diag[0]), (sub_diag, main_diag, sup_diag))
    return pivots, ratios


def substitute(sub_diag, pivots, ratios, source):
    def forward(prev_value, packed):
        sub_row, pivot_row, source_row = packed
        new_value = (source_row - sub_row * prev_value) * pivot_row
        return new_value, new_value

    _, partial_sol = lax.scan(forward, jnp.zeros_like(source[0]), (sub_diag, pivots, source))

    def backward(next_value, packed):
        ratio_row, partial_row = packed
        new_value = partial_row - ratio_row * next_value
        return new_value, new_value

    _, solved = lax.scan(backward, jnp.zeros_like(source[0]), (ratios, partial_sol), reverse=True)
    return solved


def reference(starting_sag, warmth_celsius_field, junction_charge_store, load_amperes, source_patch_bits):
    xward_wire = xward_admittance / (1.0 + warmth_scaling * (0.5 * (warmth_celsius_field[:-1] + warmth_celsius_field[1:]) - surrounding_warmth))
    yward_wire = yward_admittance / (1.0 + warmth_scaling * (0.5 * (warmth_celsius_field[:, :-1] + warmth_celsius_field[:, 1:]) - surrounding_warmth))
    blank_xcoord = jnp.zeros((1, STRIP_TRACKS), warmth_celsius_field.dtype)
    blank_ycoord = jnp.zeros((POINTS_EACH_RUN, 1), warmth_celsius_field.dtype)
    left_x = jnp.concatenate([blank_xcoord, xward_wire], 0)
    right_x = jnp.concatenate([xward_wire, blank_xcoord], 0)
    left_y = jnp.concatenate([blank_ycoord, yward_wire], 1)
    right_y = jnp.concatenate([yward_wire, blank_ycoord], 1)
    patch_indicators = jnp.repeat(jnp.repeat(source_patch_bits, PITCH, axis=0), PITCH, axis=1)
    xcoord_table = (jnp.arange(POINTS_EACH_RUN) % PITCH == 0)[:, None]
    ycoord_table = (jnp.arange(STRIP_TRACKS) % PITCH == 0)[None, :]
    semi_cushion = jnp.where(xcoord_table & ycoord_table & (patch_indicators == 1), cushion_pieces, 0.0).astype(warmth_celsius_field.dtype)
    diag_x = junction_charge_store + left_x + right_x + semi_cushion
    diag_y = junction_charge_store + left_y + right_y + semi_cushion
    pivots_x, ratios_x = factor(-left_x, diag_x, -right_x)
    pivots_y, ratios_y = factor(-left_y.T, diag_y.T, -right_y.T)

    def operate_x(field_in):
        padded = jnp.pad(field_in, ((1, 1), (0, 0)))
        return right_x * (field_in - padded[2:]) + left_x * (field_in - padded[:-2]) + semi_cushion * field_in

    def operate_y(field_in):
        padded = jnp.pad(field_in, ((0, 0), (1, 1)))
        return right_y * (field_in - padded[:, 2:]) + left_y * (field_in - padded[:, :-2]) + semi_cushion * field_in

    drop_now = starting_sag
    for step_index in range(STEPS):
        source = junction_charge_store * drop_now - operate_y(drop_now) + load_amperes[step_index]
        half_drop = substitute(-left_x, pivots_x, ratios_x, source)
        source = junction_charge_store * half_drop - operate_x(half_drop) + load_amperes[step_index]
        drop_now = substitute(-left_y.T, pivots_y, ratios_y, source.T).T
    return drop_now
```

```python
import functools

import jax
import jax.numpy as jnp
from jax import lax
from jax.experimental import pallas as pl
from jax.experimental.pallas import tpu as pltpu
from jax.sharding import PartitionSpec as P

STEPS = 2
PITCH = 32
SUB = 8

xward_admittance = 1.0
yward_admittance = 0.5
warmth_scaling = 0.004
surrounding_warmth = 25.0
cushion_pieces = 1.0

MESH = pl.DeviceIdType.MESH


def roll(x, shift):
    return pltpu.roll(x, shift % x.shape[0], 0)


def sublanes(rows=SUB, lanes=128):
    return lax.broadcasted_iota(jnp.int32, (rows, lanes), 0)


def total(x):
    for step in (4, 2, 1):
        x = x + roll(x, step)
    return x


def wire(admittance, here, there):
    return admittance / (
        1.0 + warmth_scaling * (0.5 * (here + there) - surrounding_warmth)
    )


def pcr_factor(ground, link):
    rows = ground.shape[0]
    up = link
    down = jnp.where(sublanes(rows) == 0, 0.0, roll(link, 1))
    levels = []
    step = 1
    while step < rows:
        inverse = 1.0 / (ground + up + down)
        take_up = up * roll(inverse, -step)
        take_down = down * roll(inverse, step)
        levels.append((step, take_up, take_down))
        ground = ground + take_up * roll(ground, -step) + take_down * roll(ground, step)
        up, down = take_up * roll(up, -step), take_down * roll(down, step)
        step *= 2
    return levels, 1.0 / ground


def pcr_apply(factors, source):
    levels, inverse = factors
    for step, take_up, take_down in levels:
        source = source + take_up * roll(source, -step) + take_down * roll(source, step)
    return source * inverse


def chain_order(depth):
    order, step = [], 1
    while step < depth:
        order.append([(k, k - step, k + step) for k in range(step, depth, 2 * step)])
        step *= 2
    return order


def after(first, fill):
    return jnp.where(sublanes() == SUB - 1, fill, roll(first, -1))


class Line:
    def __init__(self, ground, link):
        depth = len(ground)
        self.depth = depth
        sub = sublanes()
        own = list(ground) + [jnp.zeros_like(ground[0])]
        right = list(link)
        self.node = {}
        for level in chain_order(depth):
            for k, lo, hi in level:
                left_link, right_link = right[lo], right[k]
                inverse = 1.0 / (own[k] + left_link + right_link)
                to_lo, to_hi = left_link * inverse, right_link * inverse
                self.node[k] = (inverse, to_lo, to_hi)
                own[lo] = own[lo] + to_lo * own[k]
                own[hi] = own[hi] + to_hi * own[k]
                right[lo] = to_lo * right_link
        joined = right[0]
        held = own[0] + jnp.where(sub == 0, 0.0, roll(own[depth], 1))
        inner = sub > 0
        first_link = jnp.where(sub == 1, roll(joined, 1), 0.0)
        last_link = jnp.where(sub == SUB - 1, joined, 0.0)
        held = jnp.where(inner, held + first_link + last_link, 1.0)
        between = jnp.where(inner & (sub < SUB - 1), joined, 0.0)
        self.heads = pcr_factor(held, between)
        near = jnp.where(inner, pcr_apply(self.heads, first_link), 1.0)
        far = jnp.where(inner, pcr_apply(self.heads, last_link), 0.0)
        self.near = self.fill(near, after(near, 0.0))
        self.far = self.fill(far, after(far, 1.0))
        first = sub == 0
        bridge = jnp.where(first, joined * roll(far, -1), 0.0)
        near_ground, far_ground = self.condense(ground)
        self.coefficients = jnp.where(
            first,
            total(near_ground),
            jnp.where(sub == 1, total(far_ground), jnp.where(sub == 2, roll(bridge, 2), 0.0)),
        )

    def fill(self, first, last, source=None):
        value = {0: first, self.depth: last}
        for level in reversed(chain_order(self.depth)):
            for k, lo, hi in level:
                inverse, to_lo, to_hi = self.node[k]
                out = to_lo * value[lo] + to_hi * value[hi]
                value[k] = out if source is None else source[k] * inverse + out
        return [value[k] for k in range(self.depth)]

    def condense(self, source):
        near = [a * b for a, b in zip(self.near, source)]
        far = [a * b for a, b in zip(self.far, source)]
        while len(near) > 1:
            near = [a + b for a, b in zip(near[::2], near[1::2])]
            far = [a + b for a, b in zip(far[::2], far[1::2])]
        return near[0], far[0]

    def message(self, source):
        near, far = self.condense(source)
        return jnp.where(sublanes() < 4, near + roll(near, 4), far + roll(far, 4))

    def inside(self, source):
        sub = sublanes()
        now = list(source) + [jnp.zeros_like(source[0])]
        for level in chain_order(self.depth):
            for k, lo, hi in level:
                _, to_lo, to_hi = self.node[k]
                now[lo] = now[lo] + to_lo * now[k]
                now[hi] = now[hi] + to_hi * now[k]
        head = jnp.where(sub == 0, 0.0, now[0] + roll(now[self.depth], 1))
        first = pcr_apply(self.heads, head)
        return self.fill(first, after(first, 0.0), now)

    def weigh(self, parts, place):
        devices = len(parts)
        rows = max(SUB, devices)
        at = sublanes(rows)
        spread = [jnp.zeros((rows, 128), jnp.float32) for _ in range(3)]
        for d, part in enumerate(parts):
            for r in range(3):
                spread[r] = jnp.where(at == d, part[r : r + 1], spread[r])
        ground = spread[0] + roll(spread[1], 1)
        ground = jnp.where(at < devices, ground, 1.0)
        factors = pcr_factor(ground, spread[2])
        upper = sublanes() < 4
        blank = jnp.zeros((1, 128), jnp.float32)
        self.weights = []
        for kept in (place, place + 1):
            unit = jnp.where((at == kept) & (at < devices), 1.0, 0.0)
            row = pcr_apply(factors, unit)
            self.weights.append(
                [
                    jnp.where(upper, row[d : d + 1], row[d + 1 : d + 2] if d + 1 < devices else blank)
                    for d in range(devices)
                ]
            )

    def finish(self, messages, inside):
        own, next_one = (
            total(functools.reduce(jnp.add, [w * m for w, m in zip(weights, messages)]))
            for weights in self.weights
        )
        return [
            u + near * own + far * next_one
            for u, near, far in zip(inside, self.near, self.far)
        ]


class Exchange:
    def __init__(self, axis, devices, mine, slots, send_sem, recv_sem):
        place = lax.axis_index(axis)
        self.copies = [
            pltpu.make_async_remote_copy(
                src_ref=mine,
                dst_ref=slots.at[place],
                send_sem=send_sem.at[ahead - 1],
                recv_sem=recv_sem.at[ahead - 1],
                device_id={axis: lax.rem(place + ahead, devices)},
                device_id_type=MESH,
            )
            for ahead in range(1, devices)
        ]
        self.place, self.devices, self.mine, self.slots = place, devices, mine, slots

    def start(self, value):
        self.mine[...] = value
        for copy in self.copies:
            copy.start()

    def arrived(self):
        for copy in self.copies:
            copy.wait_recv()
        return [
            jnp.where(self.place == d, self.mine[...], self.slots[d]) for d in range(self.devices)
        ]

    def close(self):
        for copy in self.copies:
            copy.wait_send()


def kernel(
    count_x, count_y,
    sag_ref, warmth_ref, store_ref, load_ref, flag_ref,
    out_ref,
    turn_ref, halo_x, halo_y, edge_y,
    mine_x0, slots_x0, mine_x1, slots_x1,
    mine_yc, slots_yc, mine_y0, slots_y0, mine_y1, slots_y1,
    halo_send, halo_recv,
    x0_send, x0_recv, x1_send, x1_recv,
    yc_send, yc_recv, y0_send, y0_recv, y1_send, y1_recv,
):
    place_x = lax.axis_index("gx")
    place_y = lax.axis_index("gy")
    rows, cols = sag_ref.shape
    depth_x, depth_y = rows // SUB, cols // SUB
    sub = sublanes()
    lane = lax.broadcasted_iota(jnp.int32, (SUB, 128), 1)

    halo_x[...] = jnp.zeros_like(halo_x)
    halo_y[...] = jnp.zeros_like(halo_y)
    barrier = pltpu.get_barrier_semaphore()
    for axis, place, devices in (("gx", place_x, count_x), ("gy", place_y, count_y)):
        for ahead in range(1, devices):
            pl.semaphore_signal(
                barrier, inc=1,
                device_id={axis: lax.rem(place + ahead, devices)}, device_id_type=MESH,
            )

    def split(ref, depth):
        return [ref[pl.ds(k, SUB, stride=depth), :] for k in range(depth)]

    def to_y(parts):
        turn_ref[...] = jnp.concatenate(parts, 0).T
        return split(turn_ref, depth_y)

    def to_x(parts):
        for k, part in enumerate(parts):
            turn_ref[pl.ds(k, SUB, stride=depth_y), :] = part
        turned = turn_ref[...].T
        return [turned[SUB * k : SUB * k + SUB] for k in range(depth_x)]

    warmth_x = split(warmth_ref, depth_x)
    warmth_y = to_y(warmth_x)
    sag_y = to_y(split(sag_ref, depth_x))
    end_y = depth_y - 1
    edge_y[0] = jnp.where(sub == 0, warmth_y[0], roll(sag_y[0], 1))
    edge_y[1] = jnp.where(sub == 0, roll(warmth_y[end_y], 1), roll(sag_y[end_y], 2))

    pl.semaphore_wait(barrier, count_x - 1 + count_y - 1)

    halos = [
        (place_x > 0, place_x < count_x - 1, pltpu.make_async_remote_copy(
            src_ref=warmth_ref.at[pl.ds(0, SUB)], dst_ref=halo_x,
            send_sem=halo_send.at[0], recv_sem=halo_recv.at[0],
            device_id={"gx": lax.rem(place_x + count_x - 1, count_x)}, device_id_type=MESH)),
        (place_y > 0, place_y < count_y - 1, pltpu.make_async_remote_copy(
            src_ref=edge_y.at[0], dst_ref=halo_y.at[0],
            send_sem=halo_send.at[1], recv_sem=halo_recv.at[1],
            device_id={"gy": lax.rem(place_y + count_y - 1, count_y)}, device_id_type=MESH)),
        (place_y < count_y - 1, place_y > 0, pltpu.make_async_remote_copy(
            src_ref=edge_y.at[1], dst_ref=halo_y.at[1],
            send_sem=halo_send.at[2], recv_sem=halo_recv.at[2],
            device_id={"gy": lax.rem(place_y + 1, count_y)}, device_id_type=MESH)),
    ]
    for sends, _, copy in halos:
        pl.when(sends)(copy.start)

    store_x = split(store_ref, depth_x)
    store_y = to_y(store_x)
    cushion_x = jnp.zeros((SUB, 128), jnp.float32)
    cushion_y = jnp.zeros((SUB, 128), jnp.float32)
    for a in range(rows // PITCH):
        for b in range(cols // PITCH):
            flag = cushion_pieces * flag_ref[a, b].astype(jnp.float32)
            at_a, at_b = PITCH // depth_x * a, PITCH // depth_y * b
            cushion_x = jnp.where((sub == at_a) & (lane == PITCH * b), flag, cushion_x)
            cushion_y = jnp.where((sub == at_b) & (lane == at_a), flag, cushion_y)
    ground_x = [store_x[0] + cushion_x] + store_x[1:]
    ground_y = [store_y[0] + cushion_y] + store_y[1:]

    for _, receives, copy in halos:
        pl.when(receives)(copy.wait_recv)

    last_x = (sub == SUB - 1) & (place_x == count_x - 1)
    last_y = (sub == SUB - 1) & (place_y == count_y - 1)
    first_y = (sub == 0) & (place_y == 0)
    next_x = warmth_x[1:] + [after(warmth_x[0], halo_x[0:1])]
    link_x = [wire(xward_admittance, a, b) for a, b in zip(warmth_x, next_x)]
    link_x[-1] = jnp.where(last_x, 0.0, link_x[-1])
    next_y = warmth_y[1:] + [after(warmth_y[0], halo_y[0, 0:1])]
    link_y = [wire(yward_admittance, a, b) for a, b in zip(warmth_y, next_y)]
    link_y[-1] = jnp.where(last_y, 0.0, link_y[-1])

    next_sag = sag_y[1:] + [after(sag_y[0], halo_y[0, 1:2])]
    flow = [g * (a - b) for g, a, b in zip(link_y, sag_y, next_sag)]
    inflow = wire(yward_admittance, halo_y[1, 0:1], warmth_y[0]) * (halo_y[1, 1:2] - sag_y[0])
    inflow = jnp.where(first_y, 0.0, inflow)
    flow_in = [jnp.where(sub == 0, inflow, roll(flow[-1], 1))] + flow[:-1]
    source_y = [c * v - (o - i) for c, v, o, i in zip(store_y, sag_y, flow, flow_in)]
    source_y[0] = source_y[0] - cushion_y * sag_y[0]

    exchange_x = [
        Exchange("gx", count_x, mine_x0, slots_x0, x0_send, x0_recv),
        Exchange("gx", count_x, mine_x1, slots_x1, x1_send, x1_recv),
    ]
    share_y = Exchange("gy", count_y, mine_yc, slots_yc, yc_send, yc_recv)
    exchange_y = [
        Exchange("gy", count_y, mine_y0, slots_y0, y0_send, y0_recv),
        Exchange("gy", count_y, mine_y1, slots_y1, y1_send, y1_recv),
    ]

    line_x = Line(ground_x, link_x)
    load = [split(load_ref.at[s], depth_x) for s in range(STEPS)]
    source = [a + b for a, b in zip(to_x(source_y), load[0])]
    for s in range(STEPS):
        message = line_x.message(source)
        if s == 0:
            exchange_x[s].start(jnp.stack([message, line_x.coefficients]))
            line_y = Line(ground_y, link_y)
            share_y.start(line_y.coefficients)
        else:
            exchange_x[s].start(message)
        inside = line_x.inside(source)
        got = exchange_x[s].arrived()
        if s == 0:
            line_x.weigh([part[1] for part in got], place_x)
            got = [part[0] for part in got]
        half = line_x.finish(got, inside)
        source = [2.0 * c * h - f + q for c, h, f, q in zip(store_x, half, source, load[s])]
        source_y = to_y(source)
        exchange_y[s].start(line_y.message(source_y))
        if s == 0:
            line_y.weigh(share_y.arrived(), place_y)
        inside = line_y.inside(source_y)
        drop = line_y.finish(exchange_y[s].arrived(), inside)
        if s + 1 < STEPS:
            carried = [2.0 * c * v - f for c, v, f in zip(store_y, drop, source_y)]
            source = [a + b for a, b in zip(to_x(carried), load[s + 1])]
    for k, part in enumerate(to_x(drop)):
        out_ref[pl.ds(k, SUB, stride=depth_x), :] = part

    for exchange in exchange_x + [share_y] + exchange_y:
        exchange.close()
    for sends, _, copy in halos:
        pl.when(sends)(copy.wait_send)


def local(count_x, count_y, sag, warmth, store, load, flags):
    tile = (SUB, 128)
    vmem = pl.BlockSpec(memory_space=pltpu.VMEM)

    def buffers(devices, shape):
        return [pltpu.VMEM(shape, jnp.float32), pltpu.VMEM((devices,) + shape, jnp.float32)]

    def semaphores(devices):
        return [pltpu.SemaphoreType.DMA((devices - 1,))] * 2

    return pl.pallas_call(
        functools.partial(kernel, count_x, count_y),
        out_shape=jax.ShapeDtypeStruct(sag.shape, jnp.float32),
        in_specs=[vmem] * 4 + [pl.BlockSpec(memory_space=pltpu.SMEM)],
        out_specs=vmem,
        scratch_shapes=[
            pltpu.VMEM((sag.shape[1], sag.shape[0]), jnp.float32),
            pltpu.VMEM(tile, jnp.float32),
            pltpu.VMEM((2,) + tile, jnp.float32),
            pltpu.VMEM((2,) + tile, jnp.float32),
            *buffers(count_x, (2,) + tile),
            *buffers(count_x, tile),
            *buffers(count_y, tile),
            *buffers(count_y, tile),
            *buffers(count_y, tile),
            pltpu.SemaphoreType.DMA((3,)),
            pltpu.SemaphoreType.DMA((3,)),
            *semaphores(count_x),
            *semaphores(count_x),
            *semaphores(count_y),
            *semaphores(count_y),
            *semaphores(count_y),
        ],
        compiler_params=pltpu.CompilerParams(
            collective_id=0, has_side_effects=True, vmem_limit_bytes=16 * 2**20
        ),
    )(sag, warmth, store, load, flags)


def solution(mesh):
    return jax.shard_map(
        functools.partial(local, mesh.shape["gx"], mesh.shape["gy"]),
        mesh=mesh,
        in_specs=(P("gx", "gy"), P("gx", "gy"), P("gx", "gy"), P(None, "gx", "gy"), P("gx", "gy")),
        out_specs=P("gx", "gy"),
        check_vma=False,
    )
```

```python
import functools

import jax
import jax.numpy as jnp
from jax import lax
from jax.experimental import pallas as pl
from jax.experimental.pallas import tpu as pltpu
from jax.sharding import PartitionSpec as P

STEPS = 2
PITCH = 32
SUB = 8
SHORT = 1e20

xward_admittance = 1.0
yward_admittance = 0.5
warmth_scaling = 0.004
surrounding_warmth = 25.0
cushion_pieces = 1.0

MESH = pl.DeviceIdType.MESH


def roll(x, shift):
    return pltpu.roll(x, shift % x.shape[0], 0)


def sublanes(rows=SUB, lanes=128):
    return lax.broadcasted_iota(jnp.int32, (rows, lanes), 0)


def total(x):
    for step in (4, 2, 1):
        x = x + roll(x, step)
    return x


def wire(admittance, here, there):
    return admittance / (
        1.0 + warmth_scaling * (0.5 * (here + there) - surrounding_warmth)
    )


def pcr_factor(ground, link):
    rows = ground.shape[0]
    up = link
    down = jnp.where(sublanes(rows) == 0, 0.0, roll(link, 1))
    levels = []
    step = 1
    while step < rows:
        inverse = 1.0 / (ground + up + down)
        take_up = up * roll(inverse, -step)
        take_down = down * roll(inverse, step)
        levels.append((step, take_up, take_down))
        ground = ground + take_up * roll(ground, -step) + take_down * roll(ground, step)
        up, down = take_up * roll(up, -step), take_down * roll(down, step)
        step *= 2
    return levels, 1.0 / ground


def pcr_apply(factors, source):
    levels, inverse = factors
    for step, take_up, take_down in levels:
        source = source + take_up * roll(source, -step) + take_down * roll(source, step)
    return source * inverse


def chain_order(depth):
    order, step = [], 1
    while step < depth:
        order.append([(k, k - step, k + step) for k in range(step, depth, 2 * step)])
        step *= 2
    return order


def after(first, fill):
    return jnp.where(sublanes() == SUB - 1, fill, roll(first, -1))


class Line:
    def __init__(self, ground, link, warmth, admittance):
        depth = len(ground)
        self.depth = depth
        sub = sublanes()
        own = list(ground) + [jnp.zeros_like(ground[0])]
        right = list(link)
        right[-1] = jnp.where(sub == SUB - 1, SHORT, right[-1])
        self.admittance = admittance
        self.node = {}
        for level in chain_order(depth):
            for k, lo, hi in level:
                left_link, right_link = right[lo], right[k]
                inverse = 1.0 / (own[k] + left_link + right_link)
                to_lo, to_hi = left_link * inverse, right_link * inverse
                self.node[k] = (inverse, to_lo, to_hi)
                own[lo] = own[lo] + to_lo * own[k]
                own[hi] = own[hi] + to_hi * own[k]
                right[lo] = to_lo * right_link
        joined = right[0]
        held = own[0] + jnp.where(sub == 0, 0.0, roll(own[depth], 1))
        inner = sub > 0
        first_link = jnp.where(sub == 1, roll(joined, 1), 0.0)
        last_link = jnp.where(sub == SUB - 1, joined, 0.0)
        held = jnp.where(inner, held + first_link + last_link, 1.0)
        between = jnp.where(inner & (sub < SUB - 1), joined, 0.0)
        self.heads = pcr_factor(held, between)
        near = jnp.where(inner, pcr_apply(self.heads, first_link), 1.0)
        far = jnp.where(inner, pcr_apply(self.heads, last_link), 0.0)
        self.near = self.fill(near, after(near, 0.0))
        self.far = self.fill(far, after(far, 1.0))
        first = sub == 0
        bridge = jnp.where(first, joined * roll(far, -1), 0.0)
        near_ground, far_ground = self.condense(ground)
        rows = [total(near_ground), total(far_ground), roll(bridge, 2)]
        rows += [roll(warmth[0], 3), roll(warmth[-1], 5)]
        self.coefficients = jnp.zeros_like(ground[0])
        for r, row in enumerate(rows):
            self.coefficients = jnp.where(sub == r, row, self.coefficients)

    def fill(self, first, last, source=None):
        value = {0: first, self.depth: last}
        for level in reversed(chain_order(self.depth)):
            for k, lo, hi in level:
                inverse, to_lo, to_hi = self.node[k]
                out = to_lo * value[lo] + to_hi * value[hi]
                value[k] = out if source is None else source[k] * inverse + out
        return [value[k] for k in range(self.depth)]

    def condense(self, source):
        near = [a * b for a, b in zip(self.near, source)]
        far = [a * b for a, b in zip(self.far, source)]
        while len(near) > 1:
            near = [a + b for a, b in zip(near[::2], near[1::2])]
            far = [a + b for a, b in zip(far[::2], far[1::2])]
        return near[0], far[0]

    def message(self, source):
        near, far = self.condense(source)
        return jnp.where(sublanes() < 4, near + roll(near, 4), far + roll(far, 4))

    def inside(self, source):
        sub = sublanes()
        now = list(source) + [jnp.zeros_like(source[0])]
        for level in chain_order(self.depth):
            for k, lo, hi in level:
                _, to_lo, to_hi = self.node[k]
                now[lo] = now[lo] + to_lo * now[k]
                now[hi] = now[hi] + to_hi * now[k]
        head = jnp.where(sub == 0, 0.0, now[0] + roll(now[self.depth], 1))
        first = pcr_apply(self.heads, head)
        return self.fill(first, after(first, 0.0), now)

    def weigh(self, parts, place):
        devices = len(parts)
        rows = max(SUB, 2 * devices)
        at = sublanes(rows)
        ground = jnp.ones((rows, 128), jnp.float32)
        link = jnp.zeros((rows, 128), jnp.float32)
        for d, part in enumerate(parts):
            ground = jnp.where(at == 2 * d, part[0:1], ground)
            ground = jnp.where(at == 2 * d + 1, part[1:2], ground)
            link = jnp.where(at == 2 * d, part[2:3], link)
            if d + 1 < devices:
                between = wire(self.admittance, part[4:5], parts[d + 1][3:4])
                link = jnp.where(at == 2 * d + 1, between, link)
        factors = pcr_factor(ground, link)
        upper = sublanes() < 4
        self.weights = []
        for kept in (2 * place, 2 * place + 1):
            row = pcr_apply(factors, jnp.where(at == kept, 1.0, 0.0))
            self.weights.append(
                [
                    jnp.where(upper, row[2 * d : 2 * d + 1], row[2 * d + 1 : 2 * d + 2])
                    for d in range(devices)
                ]
            )

    def finish(self, messages, inside):
        first, last = (
            total(functools.reduce(jnp.add, [w * m for w, m in zip(weights, messages)]))
            for weights in self.weights
        )
        return [
            u + near * first + far * last
            for u, near, far in zip(inside, self.near, self.far)
        ]


class Exchange:
    def __init__(self, axis, devices, mine, slots, send_sem, recv_sem):
        place = lax.axis_index(axis)
        self.copies = [
            pltpu.make_async_remote_copy(
                src_ref=mine,
                dst_ref=slots.at[place],
                send_sem=send_sem.at[ahead - 1],
                recv_sem=recv_sem.at[ahead - 1],
                device_id={axis: lax.rem(place + ahead, devices)},
                device_id_type=MESH,
            )
            for ahead in sorted(range(1, devices), key=lambda a: -min(a, devices - a))
        ]
        self.place, self.devices, self.mine, self.slots = place, devices, mine, slots

    def start(self, value):
        self.mine[...] = value
        for copy in self.copies:
            copy.start()

    def arrived(self):
        for copy in self.copies:
            copy.wait_recv()
        return [
            jnp.where(self.place == d, self.mine[...], self.slots[d]) for d in range(self.devices)
        ]

    def close(self):
        for copy in self.copies:
            copy.wait_send()


def kernel(
    count_x, count_y,
    sag_hbm, warmth_hbm, store_hbm, load_hbm, flag_hbm,
    out_ref,
    sag_ref, warmth_ref, store_ref, load_ref, flag_ref, fetch_sem,
    turn_ref, halo_y, edge_y,
    mine_xc, slots_xc, mine_x0, slots_x0, mine_x1, slots_x1,
    mine_yc, slots_yc, mine_y0, slots_y0, mine_y1, slots_y1,
    halo_send, halo_recv,
    xc_send, xc_recv, x0_send, x0_recv, x1_send, x1_recv,
    yc_send, yc_recv, y0_send, y0_recv, y1_send, y1_recv,
):
    place_x = lax.axis_index("gx")
    place_y = lax.axis_index("gy")
    rows, cols = sag_ref.shape
    depth_x, depth_y = rows // SUB, cols // SUB
    sub = sublanes()
    lane = lax.broadcasted_iota(jnp.int32, (SUB, 128), 1)

    fetches = [
        pltpu.make_async_copy(src, dst, fetch_sem.at[k])
        for k, (src, dst) in enumerate([
            (warmth_hbm, warmth_ref), (sag_hbm, sag_ref), (store_hbm, store_ref),
            (flag_hbm, flag_ref), (load_hbm, load_ref),
        ])
    ]
    for fetch in fetches:
        fetch.start()
    halo_y[...] = jnp.zeros_like(halo_y)
    barrier = pltpu.get_barrier_semaphore()
    for axis, place, devices in (("gx", place_x, count_x), ("gy", place_y, count_y)):
        for ahead in range(1, devices):
            pl.semaphore_signal(
                barrier, inc=1,
                device_id={axis: lax.rem(place + ahead, devices)}, device_id_type=MESH,
            )

    def split(ref, depth):
        return [ref[pl.ds(k, SUB, stride=depth), :] for k in range(depth)]

    def to_y(parts):
        turn_ref[...] = jnp.concatenate(parts, 0).T
        return split(turn_ref, depth_y)

    def to_x(parts):
        for k, part in enumerate(parts):
            turn_ref[pl.ds(k, SUB, stride=depth_y), :] = part
        turned = turn_ref[...].T
        return [turned[SUB * k : SUB * k + SUB] for k in range(depth_x)]

    fetches[0].wait()
    fetches[1].wait()
    warmth_x = split(warmth_ref, depth_x)
    warmth_y = to_y(warmth_x)
    sag_y = to_y(split(sag_ref, depth_x))
    end_y = depth_y - 1
    edge_y[0] = jnp.where(sub == 0, warmth_y[0], roll(sag_y[0], 1))
    edge_y[1] = jnp.where(sub == 0, roll(warmth_y[end_y], 1), roll(sag_y[end_y], 2))

    pl.semaphore_wait(barrier, count_x - 1 + count_y - 1)

    halos = [
        (place_y > 0, place_y < count_y - 1, pltpu.make_async_remote_copy(
            src_ref=edge_y.at[0], dst_ref=halo_y.at[0],
            send_sem=halo_send.at[0], recv_sem=halo_recv.at[0],
            device_id={"gy": lax.rem(place_y + count_y - 1, count_y)}, device_id_type=MESH)),
        (place_y < count_y - 1, place_y > 0, pltpu.make_async_remote_copy(
            src_ref=edge_y.at[1], dst_ref=halo_y.at[1],
            send_sem=halo_send.at[1], recv_sem=halo_recv.at[1],
            device_id={"gy": lax.rem(place_y + 1, count_y)}, device_id_type=MESH)),
    ]
    for sends, _, copy in halos:
        pl.when(sends)(copy.start)

    fetches[2].wait()
    fetches[3].wait()
    store_x = split(store_ref, depth_x)
    store_y = to_y(store_x)
    cushion_x = jnp.zeros((SUB, 128), jnp.float32)
    cushion_y = jnp.zeros((SUB, 128), jnp.float32)
    for a in range(rows // PITCH):
        for b in range(cols // PITCH):
            flag = cushion_pieces * flag_ref[a, b].astype(jnp.float32)
            at_a, at_b = PITCH // depth_x * a, PITCH // depth_y * b
            cushion_x = jnp.where((sub == at_a) & (lane == PITCH * b), flag, cushion_x)
            cushion_y = jnp.where((sub == at_b) & (lane == at_a), flag, cushion_y)
    ground_x = [store_x[0] + cushion_x] + store_x[1:]
    ground_y = [store_y[0] + cushion_y] + store_y[1:]

    next_x = warmth_x[1:] + [roll(warmth_x[0], -1)]
    link_x = [wire(xward_admittance, a, b) for a, b in zip(warmth_x, next_x)]
    line_x = Line(ground_x, link_x, warmth_x, xward_admittance)
    share_x = Exchange("gx", count_x, mine_xc, slots_xc, xc_send, xc_recv)
    share_x.start(line_x.coefficients)

    for _, receives, copy in halos:
        pl.when(receives)(copy.wait_recv)

    last_y = (sub == SUB - 1) & (place_y == count_y - 1)
    first_y = (sub == 0) & (place_y == 0)
    next_y = warmth_y[1:] + [after(warmth_y[0], halo_y[0, 0:1])]
    link_y = [wire(yward_admittance, a, b) for a, b in zip(warmth_y, next_y)]
    link_y[-1] = jnp.where(last_y, 0.0, link_y[-1])
    next_sag = sag_y[1:] + [after(sag_y[0], halo_y[0, 1:2])]
    flow = [g * (a - b) for g, a, b in zip(link_y, sag_y, next_sag)]
    inflow = wire(yward_admittance, halo_y[1, 0:1], warmth_y[0]) * (halo_y[1, 1:2] - sag_y[0])
    inflow = jnp.where(first_y, 0.0, inflow)
    flow_in = [jnp.where(sub == 0, inflow, roll(flow[-1], 1))] + flow[:-1]
    source_y = [c * v - (o - i) for c, v, o, i in zip(store_y, sag_y, flow, flow_in)]
    source_y[0] = source_y[0] - cushion_y * sag_y[0]

    exchange_x = [
        Exchange("gx", count_x, mine_x0, slots_x0, x0_send, x0_recv),
        Exchange("gx", count_x, mine_x1, slots_x1, x1_send, x1_recv),
    ]
    share_y = Exchange("gy", count_y, mine_yc, slots_yc, yc_send, yc_recv)
    exchange_y = [
        Exchange("gy", count_y, mine_y0, slots_y0, y0_send, y0_recv),
        Exchange("gy", count_y, mine_y1, slots_y1, y1_send, y1_recv),
    ]

    fetches[4].wait()
    load = [split(load_ref.at[s], depth_x) for s in range(STEPS)]
    source = [a + b for a, b in zip(to_x(source_y), load[0])]
    for s in range(STEPS):
        exchange_x[s].start(line_x.message(source))
        if s == 0:
            line_x.weigh(share_x.arrived(), place_x)
            line_y = Line(ground_y, link_y, warmth_y, yward_admittance)
            share_y.start(line_y.coefficients)
        inside = line_x.inside(source)
        half = line_x.finish(exchange_x[s].arrived(), inside)
        source = [2.0 * c * h - f + q for c, h, f, q in zip(store_x, half, source, load[s])]
        source_y = to_y(source)
        exchange_y[s].start(line_y.message(source_y))
        if s == 0:
            line_y.weigh(share_y.arrived(), place_y)
        inside = line_y.inside(source_y)
        drop = line_y.finish(exchange_y[s].arrived(), inside)
        if s + 1 < STEPS:
            carried = [2.0 * c * v - f for c, v, f in zip(store_y, drop, source_y)]
            source = [a + b for a, b in zip(to_x(carried), load[s + 1])]
    for k, part in enumerate(to_x(drop)):
        out_ref[pl.ds(k, SUB, stride=depth_x), :] = part

    for exchange in exchange_x + [share_x, share_y] + exchange_y:
        exchange.close()
    for sends, _, copy in halos:
        pl.when(sends)(copy.wait_send)


def local(count_x, count_y, sag, warmth, store, load, flags):
    tile = (SUB, 128)
    vmem = pl.BlockSpec(memory_space=pltpu.VMEM)

    def buffers(devices, shape):
        return [pltpu.VMEM(shape, jnp.float32), pltpu.VMEM((devices,) + shape, jnp.float32)]

    def semaphores(devices):
        return [pltpu.SemaphoreType.DMA((devices - 1,))] * 2

    return pl.pallas_call(
        functools.partial(kernel, count_x, count_y),
        out_shape=pltpu.VMEM(sag.shape, jnp.float32),
        in_specs=[pl.BlockSpec(memory_space=pltpu.HBM)] * 5,
        out_specs=vmem,
        scratch_shapes=[
            *(pltpu.VMEM(x.shape, jnp.float32) for x in (sag, warmth, store, load)),
            pltpu.SMEM(flags.shape, jnp.int32),
            pltpu.SemaphoreType.DMA((5,)),
            pltpu.VMEM((sag.shape[1], sag.shape[0]), jnp.float32),
            pltpu.VMEM((2,) + tile, jnp.float32),
            pltpu.VMEM((2,) + tile, jnp.float32),
            *buffers(count_x, tile),
            *buffers(count_x, tile),
            *buffers(count_x, tile),
            *buffers(count_y, tile),
            *buffers(count_y, tile),
            *buffers(count_y, tile),
            pltpu.SemaphoreType.DMA((2,)),
            pltpu.SemaphoreType.DMA((2,)),
            *semaphores(count_x),
            *semaphores(count_x),
            *semaphores(count_x),
            *semaphores(count_y),
            *semaphores(count_y),
            *semaphores(count_y),
        ],
        compiler_params=pltpu.CompilerParams(
            collective_id=0, has_side_effects=True, vmem_limit_bytes=16 * 2**20
        ),
    )(*(pltpu.with_memory_space_constraint(x, pltpu.HBM) for x in (sag, warmth, store, load, flags)))


def solution(mesh):
    return jax.shard_map(
        functools.partial(local, mesh.shape["gx"], mesh.shape["gy"]),
        mesh=mesh,
        in_specs=(P("gx", "gy"), P("gx", "gy"), P("gx", "gy"), P(None, "gx", "gy"), P("gx", "gy")),
        out_specs=P("gx", "gy"),
        check_vma=False,
    )
```

```python
import functools

import jax
import jax.numpy as jnp
from jax import lax
from jax.experimental import pallas as pl
from jax.experimental.pallas import tpu as pltpu
from jax.sharding import PartitionSpec as P

STEPS = 2
PITCH = 32
SUB = 8
SHORT = 1e20

xward_admittance = 1.0
yward_admittance = 0.5
warmth_scaling = 0.004
surrounding_warmth = 25.0
cushion_pieces = 1.0

MESH = pl.DeviceIdType.MESH


def roll(x, shift):
    return pltpu.roll(x, shift % x.shape[0], 0)


def sublanes(rows=SUB, lanes=128):
    return lax.broadcasted_iota(jnp.int32, (rows, lanes), 0)


def total(x):
    for step in (4, 2, 1):
        x = x + roll(x, step)
    return x


def both(pair):
    return jnp.broadcast_to(pair[0:1] + pair[1:2], (SUB, 128))


def wire(admittance, here, there):
    return admittance / (
        1.0 + warmth_scaling * (0.5 * (here + there) - surrounding_warmth)
    )


def pcr_factor(ground, link):
    rows = ground.shape[0]
    up = link
    down = jnp.where(sublanes(rows) == 0, 0.0, roll(link, 1))
    levels = []
    step = 1
    while step < rows:
        inverse = 1.0 / (ground + up + down)
        take_up = up * roll(inverse, -step)
        take_down = down * roll(inverse, step)
        levels.append((step, take_up, take_down))
        ground = ground + take_up * roll(ground, -step) + take_down * roll(ground, step)
        up, down = take_up * roll(up, -step), take_down * roll(down, step)
        step *= 2
    return levels, 1.0 / ground


def pcr_apply(factors, source):
    levels, inverse = factors
    for step, take_up, take_down in levels:
        source = source + take_up * roll(source, -step) + take_down * roll(source, step)
    return source * inverse


def chain_order(depth):
    order, step = [], 1
    while step < depth:
        order.append([(k, k - step, k + step) for k in range(step, depth, 2 * step)])
        step *= 2
    return order


def after(first, fill):
    return jnp.where(sublanes() == SUB - 1, fill, roll(first, -1))


class Line:
    def __init__(self, ground, link, warmth, admittance):
        depth = len(ground)
        self.depth = depth
        sub = sublanes()
        own = list(ground) + [jnp.zeros_like(ground[0])]
        right = list(link)
        right[-1] = jnp.where(sub == SUB - 1, SHORT, right[-1])
        self.admittance = admittance
        self.node = {}
        for level in chain_order(depth):
            for k, lo, hi in level:
                left_link, right_link = right[lo], right[k]
                inverse = 1.0 / (own[k] + left_link + right_link)
                to_lo, to_hi = left_link * inverse, right_link * inverse
                self.node[k] = (inverse, to_lo, to_hi)
                own[lo] = own[lo] + to_lo * own[k]
                own[hi] = own[hi] + to_hi * own[k]
                right[lo] = to_lo * right_link
        joined = right[0]
        held = own[0] + jnp.where(sub == 0, 0.0, roll(own[depth], 1))
        inner = sub > 0
        first_link = jnp.where(sub == 1, roll(joined, 1), 0.0)
        last_link = jnp.where(sub == SUB - 1, joined, 0.0)
        held = jnp.where(inner, held + first_link + last_link, 1.0)
        between = jnp.where(inner & (sub < SUB - 1), joined, 0.0)
        self.heads = pcr_factor(held, between)
        near = jnp.where(inner, pcr_apply(self.heads, first_link), 1.0)
        far = jnp.where(inner, pcr_apply(self.heads, last_link), 0.0)
        self.near = self.fill(near, after(near, 0.0))
        self.far = self.fill(far, after(far, 1.0))
        first = sub == 0
        bridge = jnp.where(first, joined * roll(far, -1), 0.0)
        near_ground, far_ground = self.condense(ground)
        rows = [total(near_ground), total(far_ground), roll(bridge, 2)]
        rows += [roll(warmth[0], 3), roll(warmth[-1], 5)]
        self.coefficients = jnp.zeros_like(ground[0])
        for r, row in enumerate(rows):
            self.coefficients = jnp.where(sub == r, row, self.coefficients)

    def fill(self, first, last, source=None):
        value = {0: first, self.depth: last}
        for level in reversed(chain_order(self.depth)):
            for k, lo, hi in level:
                inverse, to_lo, to_hi = self.node[k]
                out = to_lo * value[lo] + to_hi * value[hi]
                value[k] = out if source is None else source[k] * inverse + out
        return [value[k] for k in range(self.depth)]

    def condense(self, source):
        near = [a * b for a, b in zip(self.near, source)]
        far = [a * b for a, b in zip(self.far, source)]
        while len(near) > 1:
            near = [a + b for a, b in zip(near[::2], near[1::2])]
            far = [a + b for a, b in zip(far[::2], far[1::2])]
        return near[0], far[0]

    def message(self, source):
        near, far = self.condense(source)
        half = jnp.where(sublanes() < 4, near + roll(near, 4), far + roll(far, 4))
        half = half + roll(half, -2)
        half = half + roll(half, -1)
        return half[0:1], half[4:5]

    def inside(self, source):
        sub = sublanes()
        now = list(source) + [jnp.zeros_like(source[0])]
        for level in chain_order(self.depth):
            for k, lo, hi in level:
                _, to_lo, to_hi = self.node[k]
                now[lo] = now[lo] + to_lo * now[k]
                now[hi] = now[hi] + to_hi * now[k]
        head = jnp.where(sub == 0, 0.0, now[0] + roll(now[self.depth], 1))
        first = pcr_apply(self.heads, head)
        return self.fill(first, after(first, 0.0), now)

    def weigh(self, parts, place):
        devices = len(parts)
        rows = max(SUB, 2 * devices)
        at = sublanes(rows)
        ground = jnp.ones((rows, 128), jnp.float32)
        link = jnp.zeros((rows, 128), jnp.float32)
        for d, part in enumerate(parts):
            ground = jnp.where(at == 2 * d, part[0:1], ground)
            ground = jnp.where(at == 2 * d + 1, part[1:2], ground)
            link = jnp.where(at == 2 * d, part[2:3], link)
            if d + 1 < devices:
                between = wire(self.admittance, part[4:5], parts[d + 1][3:4])
                link = jnp.where(at == 2 * d + 1, between, link)
        factors = pcr_factor(ground, link)
        self.weights = []
        for kept in (2 * place, 2 * place + 1):
            row = pcr_apply(factors, jnp.where(at == kept, 1.0, 0.0))
            self.weights.append([row[2 * d : 2 * d + 2] for d in range(devices)])

    def finish(self, messages, inside):
        first, last = (
            both(functools.reduce(jnp.add, [w * m for w, m in zip(weights, messages)]))
            for weights in self.weights
        )
        return [
            u + near * first + far * last
            for u, near, far in zip(inside, self.near, self.far)
        ]


class Exchange:
    def __init__(self, axis, devices, mine, slots, send_sem, recv_sem):
        place = lax.axis_index(axis)
        self.copies = [
            pltpu.make_async_remote_copy(
                src_ref=mine,
                dst_ref=slots.at[place],
                send_sem=send_sem,
                recv_sem=recv_sem,
                device_id={axis: lax.rem(place + ahead, devices)},
                device_id_type=MESH,
            )
            for ahead in sorted(range(1, devices), key=lambda a: -min(a, devices - a))
        ]
        self.place, self.devices, self.mine, self.slots = place, devices, mine, slots
        every = slots.at[pl.ds(0, devices - 1)]
        self.received = pltpu.make_async_copy(every, every, recv_sem)
        self.sent = pltpu.make_async_copy(every, every, send_sem)

    def start(self, value):
        if isinstance(value, tuple):
            for r, row in enumerate(value):
                self.mine[r : r + 1, :] = row
        else:
            self.mine[...] = value
        for copy in self.copies:
            copy.start()

    def arrived(self):
        self.received.wait()
        return [
            jnp.where(self.place == d, self.mine[...], self.slots[d]) for d in range(self.devices)
        ]

    def close(self):
        self.sent.wait()


def kernel(
    count_x, count_y,
    sag_hbm, warmth_hbm, store_hbm, load_hbm, flag_hbm,
    out_ref,
    sag_ref, warmth_ref, store_ref, load_ref, flag_ref, fetch_sem,
    turn_ref, halo_y, edge_y,
    mine_xc, slots_xc, mine_x0, slots_x0, mine_x1, slots_x1,
    mine_yc, slots_yc, mine_y0, slots_y0, mine_y1, slots_y1,
    halo_send, halo_recv,
    xc_send, xc_recv, x0_send, x0_recv, x1_send, x1_recv,
    yc_send, yc_recv, y0_send, y0_recv, y1_send, y1_recv,
):
    place_x = lax.axis_index("gx")
    place_y = lax.axis_index("gy")
    rows, cols = sag_ref.shape
    depth_x, depth_y = rows // SUB, cols // SUB
    sub = sublanes()
    lane = lax.broadcasted_iota(jnp.int32, (SUB, 128), 1)

    fetches = [
        pltpu.make_async_copy(src, dst, fetch_sem.at[k])
        for k, (src, dst) in enumerate([
            (warmth_hbm, warmth_ref), (sag_hbm, sag_ref), (store_hbm, store_ref),
            (flag_hbm, flag_ref), (load_hbm, load_ref),
        ])
    ]
    for fetch in fetches:
        fetch.start()
    halo_y[...] = jnp.zeros_like(halo_y)
    barrier = pltpu.get_barrier_semaphore()
    for axis, place, devices in (("gx", place_x, count_x), ("gy", place_y, count_y)):
        for ahead in range(1, devices):
            pl.semaphore_signal(
                barrier, inc=1,
                device_id={axis: lax.rem(place + ahead, devices)}, device_id_type=MESH,
            )

    def split(ref, depth):
        return [ref[pl.ds(k, SUB, stride=depth), :] for k in range(depth)]

    def to_y(parts):
        turn_ref[...] = jnp.concatenate(parts, 0).T
        return split(turn_ref, depth_y)

    def to_x(parts):
        for k, part in enumerate(parts):
            turn_ref[pl.ds(k, SUB, stride=depth_y), :] = part
        turned = turn_ref[...].T
        return [turned[SUB * k : SUB * k + SUB] for k in range(depth_x)]

    fetches[0].wait()
    fetches[1].wait()
    warmth_x = split(warmth_ref, depth_x)
    warmth_y = to_y(warmth_x)
    sag_y = to_y(split(sag_ref, depth_x))
    end_y = depth_y - 1
    edge_y[0] = jnp.where(sub == 0, warmth_y[0], roll(sag_y[0], 1))
    edge_y[1] = jnp.where(sub == 0, roll(warmth_y[end_y], 1), roll(sag_y[end_y], 2))

    pl.semaphore_wait(barrier, count_x - 1 + count_y - 1)

    halos = [
        (place_y > 0, place_y < count_y - 1, pltpu.make_async_remote_copy(
            src_ref=edge_y.at[0], dst_ref=halo_y.at[0],
            send_sem=halo_send.at[0], recv_sem=halo_recv.at[0],
            device_id={"gy": lax.rem(place_y + count_y - 1, count_y)}, device_id_type=MESH)),
        (place_y < count_y - 1, place_y > 0, pltpu.make_async_remote_copy(
            src_ref=edge_y.at[1], dst_ref=halo_y.at[1],
            send_sem=halo_send.at[1], recv_sem=halo_recv.at[1],
            device_id={"gy": lax.rem(place_y + 1, count_y)}, device_id_type=MESH)),
    ]
    for sends, _, copy in halos:
        pl.when(sends)(copy.start)

    fetches[2].wait()
    fetches[3].wait()
    store_x = split(store_ref, depth_x)
    store_y = to_y(store_x)
    cushion_x = jnp.zeros((SUB, 128), jnp.float32)
    cushion_y = jnp.zeros((SUB, 128), jnp.float32)
    for a in range(rows // PITCH):
        for b in range(cols // PITCH):
            flag = cushion_pieces * flag_ref[a, b].astype(jnp.float32)
            at_a, at_b = PITCH // depth_x * a, PITCH // depth_y * b
            cushion_x = jnp.where((sub == at_a) & (lane == PITCH * b), flag, cushion_x)
            cushion_y = jnp.where((sub == at_b) & (lane == at_a), flag, cushion_y)
    ground_x = [store_x[0] + cushion_x] + store_x[1:]
    ground_y = [store_y[0] + cushion_y] + store_y[1:]

    next_x = warmth_x[1:] + [roll(warmth_x[0], -1)]
    link_x = [wire(xward_admittance, a, b) for a, b in zip(warmth_x, next_x)]
    line_x = Line(ground_x, link_x, warmth_x, xward_admittance)
    share_x = Exchange("gx", count_x, mine_xc, slots_xc, xc_send, xc_recv)
    share_x.start(line_x.coefficients)

    for _, receives, copy in halos:
        pl.when(receives)(copy.wait_recv)

    last_y = (sub == SUB - 1) & (place_y == count_y - 1)
    first_y = (sub == 0) & (place_y == 0)
    next_y = warmth_y[1:] + [after(warmth_y[0], halo_y[0, 0:1])]
    link_y = [wire(yward_admittance, a, b) for a, b in zip(warmth_y, next_y)]
    link_y[-1] = jnp.where(last_y, 0.0, link_y[-1])
    next_sag = sag_y[1:] + [after(sag_y[0], halo_y[0, 1:2])]
    flow = [g * (a - b) for g, a, b in zip(link_y, sag_y, next_sag)]
    inflow = wire(yward_admittance, halo_y[1, 0:1], warmth_y[0]) * (halo_y[1, 1:2] - sag_y[0])
    inflow = jnp.where(first_y, 0.0, inflow)
    flow_in = [jnp.where(sub == 0, inflow, roll(flow[-1], 1))] + flow[:-1]
    source_y = [c * v - (o - i) for c, v, o, i in zip(store_y, sag_y, flow, flow_in)]
    source_y[0] = source_y[0] - cushion_y * sag_y[0]

    exchange_x = [
        Exchange("gx", count_x, mine_x0, slots_x0, x0_send, x0_recv),
        Exchange("gx", count_x, mine_x1, slots_x1, x1_send, x1_recv),
    ]
    share_y = Exchange("gy", count_y, mine_yc, slots_yc, yc_send, yc_recv)
    exchange_y = [
        Exchange("gy", count_y, mine_y0, slots_y0, y0_send, y0_recv),
        Exchange("gy", count_y, mine_y1, slots_y1, y1_send, y1_recv),
    ]

    fetches[4].wait()
    load = [split(load_ref.at[s], depth_x) for s in range(STEPS)]
    source = [a + b for a, b in zip(to_x(source_y), load[0])]
    for s in range(STEPS):
        exchange_x[s].start(line_x.message(source))
        if s == 0:
            line_x.weigh(share_x.arrived(), place_x)
            line_y = Line(ground_y, link_y, warmth_y, yward_admittance)
            share_y.start(line_y.coefficients)
        else:
            exchange_y[s - 1].close()
        inside = line_x.inside(source)
        half = line_x.finish(exchange_x[s].arrived(), inside)
        source = [2.0 * c * h - f + q for c, h, f, q in zip(store_x, half, source, load[s])]
        source_y = to_y(source)
        exchange_y[s].start(line_y.message(source_y))
        exchange_x[s].close()
        if s == 0:
            share_x.close()
            share_y.close()
            for sends, _, copy in halos:
                pl.when(sends)(copy.wait_send)
            line_y.weigh(share_y.arrived(), place_y)
        inside = line_y.inside(source_y)
        drop = line_y.finish(exchange_y[s].arrived(), inside)
        if s + 1 < STEPS:
            carried = [2.0 * c * v - f for c, v, f in zip(store_y, drop, source_y)]
            source = [a + b for a, b in zip(to_x(carried), load[s + 1])]
    for k, part in enumerate(to_x(drop)):
        out_ref[pl.ds(k, SUB, stride=depth_x), :] = part

    exchange_y[-1].close()


def local(count_x, count_y, sag, warmth, store, load, flags):
    tile, pair = (SUB, 128), (2, 128)
    vmem = pl.BlockSpec(memory_space=pltpu.VMEM)

    def buffers(devices, shape):
        return [pltpu.VMEM(shape, jnp.float32), pltpu.VMEM((devices,) + shape, jnp.float32)]

    def semaphores():
        return [pltpu.SemaphoreType.DMA] * 2

    return pl.pallas_call(
        functools.partial(kernel, count_x, count_y),
        out_shape=pltpu.VMEM(sag.shape, jnp.float32),
        in_specs=[pl.BlockSpec(memory_space=pltpu.HBM)] * 5,
        out_specs=vmem,
        scratch_shapes=[
            *(pltpu.VMEM(x.shape, jnp.float32) for x in (sag, warmth, store, load)),
            pltpu.SMEM(flags.shape, jnp.int32),
            pltpu.SemaphoreType.DMA((5,)),
            pltpu.VMEM((sag.shape[1], sag.shape[0]), jnp.float32),
            pltpu.VMEM((2,) + tile, jnp.float32),
            pltpu.VMEM((2,) + tile, jnp.float32),
            *buffers(count_x, tile),
            *buffers(count_x, pair),
            *buffers(count_x, pair),
            *buffers(count_y, tile),
            *buffers(count_y, pair),
            *buffers(count_y, pair),
            pltpu.SemaphoreType.DMA((2,)),
            pltpu.SemaphoreType.DMA((2,)),
            *(semaphores() * 6),
        ],
        compiler_params=pltpu.CompilerParams(
            collective_id=0, has_side_effects=True, vmem_limit_bytes=16 * 2**20
        ),
    )(*(pltpu.with_memory_space_constraint(x, pltpu.HBM) for x in (sag, warmth, store, load, flags)))


def solution(mesh):
    return jax.shard_map(
        functools.partial(local, mesh.shape["gx"], mesh.shape["gy"]),
        mesh=mesh,
        in_specs=(P("gx", "gy"), P("gx", "gy"), P("gx", "gy"), P(None, "gx", "gy"), P("gx", "gy")),
        out_specs=P("gx", "gy"),
        check_vma=False,
    )
```

```python
import functools

import jax
import jax.numpy as jnp
from jax import lax
from jax.experimental import pallas as pl
from jax.experimental.pallas import tpu as pltpu
from jax.sharding import PartitionSpec as P

STEPS = 2
PITCH = 32
SUB = 8
SHORT = 1e20

xward_admittance = 1.0
yward_admittance = 0.5
warmth_scaling = 0.004
surrounding_warmth = 25.0
cushion_pieces = 1.0

MESH = pl.DeviceIdType.MESH


def roll(x, shift):
    return pltpu.roll(x, shift % x.shape[0], 0)


def sublanes(rows=SUB, lanes=128):
    return lax.broadcasted_iota(jnp.int32, (rows, lanes), 0)


def total(x):
    for step in (4, 2, 1):
        x = x + roll(x, step)
    return x


def tree(parts):
    while len(parts) > 1:
        parts = [functools.reduce(jnp.add, parts[k : k + 2]) for k in range(0, len(parts), 2)]
    return parts[0]


def both(pair):
    return jnp.broadcast_to(pair[0:1] + pair[1:2], (SUB, 128))


def wire(admittance, here, there):
    return admittance / (
        1.0 + warmth_scaling * (0.5 * (here + there) - surrounding_warmth)
    )


def pcr_factor(ground, link):
    rows = ground.shape[0]
    up = link
    down = jnp.where(sublanes(rows) == 0, 0.0, roll(link, 1))
    levels = []
    step = 1
    while step < rows:
        inverse = 1.0 / (ground + up + down)
        take_up = up * roll(inverse, -step)
        take_down = down * roll(inverse, step)
        levels.append((step, take_up, take_down))
        ground = ground + take_up * roll(ground, -step) + take_down * roll(ground, step)
        up, down = take_up * roll(up, -step), take_down * roll(down, step)
        step *= 2
    return levels, 1.0 / ground


def pcr_apply(factors, source):
    levels, inverse = factors
    for step, take_up, take_down in levels:
        source = source + take_up * roll(source, -step) + take_down * roll(source, step)
    return source * inverse


def chain_order(depth):
    order, step = [], 1
    while step < depth:
        order.append([(k, k - step, k + step) for k in range(step, depth, 2 * step)])
        step *= 2
    return order


def after(first, fill):
    return jnp.where(sublanes() == SUB - 1, fill, roll(first, -1))


class Line:
    def __init__(self, ground, link, warmth, admittance):
        depth = len(ground)
        self.depth = depth
        sub = sublanes()
        own = list(ground) + [jnp.zeros_like(ground[0])]
        right = list(link)
        right[-1] = jnp.where(sub == SUB - 1, SHORT, right[-1])
        self.admittance = admittance
        self.node = {}
        for level in chain_order(depth):
            for k, lo, hi in level:
                left_link, right_link = right[lo], right[k]
                inverse = 1.0 / (own[k] + left_link + right_link)
                to_lo, to_hi = left_link * inverse, right_link * inverse
                self.node[k] = (inverse, to_lo, to_hi)
                own[lo] = own[lo] + to_lo * own[k]
                own[hi] = own[hi] + to_hi * own[k]
                right[lo] = to_lo * right_link
        joined = right[0]
        held = own[0] + jnp.where(sub == 0, 0.0, roll(own[depth], 1))
        inner = sub > 0
        first_link = jnp.where(sub == 1, roll(joined, 1), 0.0)
        last_link = jnp.where(sub == SUB - 1, joined, 0.0)
        held = jnp.where(inner, held + first_link + last_link, 1.0)
        between = jnp.where(inner & (sub < SUB - 1), joined, 0.0)
        self.heads = pcr_factor(held, between)
        near = jnp.where(inner, pcr_apply(self.heads, first_link), 1.0)
        far = jnp.where(inner, pcr_apply(self.heads, last_link), 0.0)
        self.near = self.fill(near, after(near, 0.0))
        self.far = self.fill(far, after(far, 1.0))
        first = sub == 0
        bridge = jnp.where(first, joined * roll(far, -1), 0.0)
        near_ground, far_ground = self.condense(ground)
        rows = [total(near_ground), total(far_ground), roll(bridge, 2)]
        rows += [roll(warmth[0], 3), roll(warmth[-1], 5)]
        self.coefficients = jnp.zeros_like(ground[0])
        for r, row in enumerate(rows):
            self.coefficients = jnp.where(sub == r, row, self.coefficients)

    def fill(self, first, last, source=None):
        value = {0: first, self.depth: last}
        for level in reversed(chain_order(self.depth)):
            for k, lo, hi in level:
                inverse, to_lo, to_hi = self.node[k]
                out = to_lo * value[lo] + to_hi * value[hi]
                value[k] = out if source is None else source[k] * inverse + out
        return [value[k] for k in range(self.depth)]

    def condense(self, source):
        near = [a * b for a, b in zip(self.near, source)]
        far = [a * b for a, b in zip(self.far, source)]
        while len(near) > 1:
            near = [a + b for a, b in zip(near[::2], near[1::2])]
            far = [a + b for a, b in zip(far[::2], far[1::2])]
        return near[0], far[0]

    def message(self, source):
        near, far = self.condense(source)
        half = jnp.where(sublanes() < 4, near + roll(near, 4), far + roll(far, 4))
        half = half + roll(half, -2)
        half = half + roll(half, -1)
        return half[0:1], half[4:5]

    def inside(self, source):
        sub = sublanes()
        now = list(source) + [jnp.zeros_like(source[0])]
        for level in chain_order(self.depth):
            for k, lo, hi in level:
                _, to_lo, to_hi = self.node[k]
                now[lo] = now[lo] + to_lo * now[k]
                now[hi] = now[hi] + to_hi * now[k]
        head = jnp.where(sub == 0, 0.0, now[0] + roll(now[self.depth], 1))
        first = pcr_apply(self.heads, head)
        return self.fill(first, after(first, 0.0), now)

    def weigh(self, parts, place):
        devices = len(parts)
        rows = max(SUB, 2 * devices)
        at = sublanes(rows)
        ground = jnp.ones((rows, 128), jnp.float32)
        link = jnp.zeros((rows, 128), jnp.float32)
        for d, part in enumerate(parts):
            ground = jnp.where(at == 2 * d, part[0:1], ground)
            ground = jnp.where(at == 2 * d + 1, part[1:2], ground)
            link = jnp.where(at == 2 * d, part[2:3], link)
            if d + 1 < devices:
                between = wire(self.admittance, part[4:5], parts[d + 1][3:4])
                link = jnp.where(at == 2 * d + 1, between, link)
        factors = pcr_factor(ground, link)
        self.weights = []
        for kept in (2 * place, 2 * place + 1):
            row = pcr_apply(factors, jnp.where(at == kept, 1.0, 0.0))
            self.weights.append([row[2 * d : 2 * d + 2] for d in range(devices)])

    def ends(self, messages):
        return [
            both(tree([w * m for w, m in zip(weights, messages)])) for weights in self.weights
        ]

    def response(self, scale):
        return [c * p for c, p in zip(scale, self.near)], [c * p for c, p in zip(scale, self.far)]


def respond(base, response, ends):
    first, last = ends
    return [u + (p * first + q * last) for u, p, q in zip(base, *response)]


def partner(place, turn, devices):
    if devices & (devices - 1):
        return lax.rem(place + turn + 1, devices)
    flips, bit, other = devices - 1 - turn, 1, 0
    while bit < devices:
        here = lax.rem(lax.div(place, bit), 2)
        other = other + bit * (1 - here if flips & bit else here)
        bit *= 2
    return other


class Exchange:
    def __init__(self, axis, devices, mine, slots, send_sem, recv_sem):
        place = lax.axis_index(axis)
        self.copies = [
            pltpu.make_async_remote_copy(
                src_ref=mine,
                dst_ref=slots.at[place],
                send_sem=send_sem,
                recv_sem=recv_sem,
                device_id={axis: partner(place, turn, devices)},
                device_id_type=MESH,
            )
            for turn in range(devices - 1)
        ]
        self.place, self.devices, self.mine, self.slots = place, devices, mine, slots
        every = slots.at[pl.ds(0, devices - 1)]
        self.received = pltpu.make_async_copy(every, every, recv_sem)
        self.sent = pltpu.make_async_copy(every, every, send_sem)

    def start(self, value):
        if isinstance(value, tuple):
            for r, row in enumerate(value):
                self.mine[r : r + 1, :] = row
        else:
            self.mine[...] = value
        for copy in self.copies:
            copy.start()

    def arrived(self):
        self.received.wait()
        return [
            jnp.where(self.place == d, self.mine[...], self.slots[d]) for d in range(self.devices)
        ]

    def close(self):
        self.sent.wait()


def kernel(
    count_x, count_y,
    sag_hbm, warmth_hbm, store_hbm, load_hbm, flag_hbm,
    out_ref,
    sag_ref, warmth_ref, store_ref, load_ref, flag_ref, fetch_sem,
    turn_ref, halo_y, edge_y,
    mine_xc, slots_xc, mine_x0, slots_x0, mine_x1, slots_x1,
    mine_yc, slots_yc, mine_y0, slots_y0, mine_y1, slots_y1,
    halo_send, halo_recv,
    xc_send, xc_recv, x0_send, x0_recv, x1_send, x1_recv,
    yc_send, yc_recv, y0_send, y0_recv, y1_send, y1_recv,
):
    place_x = lax.axis_index("gx")
    place_y = lax.axis_index("gy")
    rows, cols = sag_ref.shape
    depth_x, depth_y = rows // SUB, cols // SUB
    sub = sublanes()
    lane = lax.broadcasted_iota(jnp.int32, (SUB, 128), 1)

    halo_y[...] = jnp.zeros_like(halo_y)
    barrier = pltpu.get_barrier_semaphore()
    for axis, place, devices in (("gy", place_y, count_y), ("gx", place_x, count_x)):
        for turn in range(devices - 1):
            pl.semaphore_signal(
                barrier, inc=1,
                device_id={axis: partner(place, turn, devices)}, device_id_type=MESH,
            )

    fetches = [
        pltpu.make_async_copy(src, dst, fetch_sem.at[k])
        for k, (src, dst) in enumerate([
            (warmth_hbm, warmth_ref), (sag_hbm, sag_ref), (store_hbm, store_ref),
            (flag_hbm, flag_ref), (load_hbm, load_ref),
        ])
    ]
    for fetch in fetches:
        fetch.start()

    def split(ref, depth):
        return [ref[pl.ds(k, SUB, stride=depth), :] for k in range(depth)]

    def to_y(parts):
        turn_ref[...] = jnp.concatenate(parts, 0).T
        return split(turn_ref, depth_y)

    def to_x(parts):
        for k, part in enumerate(parts):
            turn_ref[pl.ds(k, SUB, stride=depth_y), :] = part
        turned = turn_ref[...].T
        return [turned[SUB * k : SUB * k + SUB] for k in range(depth_x)]

    fetches[0].wait()
    fetches[1].wait()
    warmth_x = split(warmth_ref, depth_x)
    warmth_y = to_y(warmth_x)
    sag_y = to_y(split(sag_ref, depth_x))
    end_y = depth_y - 1
    edge_y[0] = jnp.where(sub == 0, warmth_y[0], roll(sag_y[0], 1))
    edge_y[1] = jnp.where(sub == 0, roll(warmth_y[end_y], 1), roll(sag_y[end_y], 2))

    pl.semaphore_wait(barrier, count_x - 1 + count_y - 1)

    halos = [
        (place_y > 0, place_y < count_y - 1, pltpu.make_async_remote_copy(
            src_ref=edge_y.at[0], dst_ref=halo_y.at[0],
            send_sem=halo_send.at[0], recv_sem=halo_recv.at[0],
            device_id={"gy": lax.rem(place_y + count_y - 1, count_y)}, device_id_type=MESH)),
        (place_y < count_y - 1, place_y > 0, pltpu.make_async_remote_copy(
            src_ref=edge_y.at[1], dst_ref=halo_y.at[1],
            send_sem=halo_send.at[1], recv_sem=halo_recv.at[1],
            device_id={"gy": lax.rem(place_y + 1, count_y)}, device_id_type=MESH)),
    ]
    for sends, _, copy in halos:
        pl.when(sends)(copy.start)

    fetches[2].wait()
    fetches[3].wait()
    store_x = split(store_ref, depth_x)
    store_y = to_y(store_x)
    cushion_x = jnp.zeros((SUB, 128), jnp.float32)
    cushion_y = jnp.zeros((SUB, 128), jnp.float32)
    for a in range(rows // PITCH):
        for b in range(cols // PITCH):
            flag = cushion_pieces * flag_ref[a, b].astype(jnp.float32)
            at_a, at_b = PITCH // depth_x * a, PITCH // depth_y * b
            cushion_x = jnp.where((sub == at_a) & (lane == PITCH * b), flag, cushion_x)
            cushion_y = jnp.where((sub == at_b) & (lane == at_a), flag, cushion_y)
    ground_x = [store_x[0] + cushion_x] + store_x[1:]
    ground_y = [store_y[0] + cushion_y] + store_y[1:]

    next_x = warmth_x[1:] + [roll(warmth_x[0], -1)]
    link_x = [wire(xward_admittance, a, b) for a, b in zip(warmth_x, next_x)]
    line_x = Line(ground_x, link_x, warmth_x, xward_admittance)
    share_x = Exchange("gx", count_x, mine_xc, slots_xc, xc_send, xc_recv)
    share_x.start(line_x.coefficients)

    next_y = warmth_y[1:] + [roll(warmth_y[0], -1)]
    link_y = [wire(yward_admittance, a, b) for a, b in zip(warmth_y, next_y)]
    line_y = Line(ground_y, link_y, warmth_y, yward_admittance)
    share_y = Exchange("gy", count_y, mine_yc, slots_yc, yc_send, yc_recv)
    share_y.start(line_y.coefficients)
    fetches[4].wait()
    load = [split(load_ref.at[s], depth_x) for s in range(STEPS)]
    twice_x = [2.0 * c for c in store_x]
    twice_y = [2.0 * c for c in store_y]
    flow = [g * (a - b) for g, a, b in zip(link_y[:-1], sag_y[:-1], sag_y[1:])]
    kept = [c * v for c, v in zip(store_y, sag_y)]
    kept[0] = kept[0] - cushion_y * sag_y[0]
    inner = [k - (o - i) for k, o, i in zip(kept[1:-1], flow[1:], flow[:-1])]

    for _, receives, copy in halos:
        pl.when(receives)(copy.wait_recv)

    last_y = (sub == SUB - 1) & (place_y == count_y - 1)
    first_y = (sub == 0) & (place_y == 0)
    next_warmth = after(warmth_y[0], halo_y[0, 0:1])
    next_sag = after(sag_y[0], halo_y[0, 1:2])
    outflow = wire(yward_admittance, warmth_y[-1], next_warmth) * (sag_y[-1] - next_sag)
    outflow = jnp.where(last_y, 0.0, outflow)
    inflow = wire(yward_admittance, halo_y[1, 0:1], warmth_y[0]) * (halo_y[1, 1:2] - sag_y[0])
    inflow = jnp.where(first_y, 0.0, inflow)
    inflow = jnp.where(sub == 0, inflow, roll(outflow, 1))
    source_y = [kept[0] - (flow[0] - inflow), *inner, kept[-1] - (outflow - flow[-1])]

    exchange_x = [
        Exchange("gx", count_x, mine_x0, slots_x0, x0_send, x0_recv),
        Exchange("gx", count_x, mine_x1, slots_x1, x1_send, x1_recv),
    ]
    exchange_y = [
        Exchange("gy", count_y, mine_y0, slots_y0, y0_send, y0_recv),
        Exchange("gy", count_y, mine_y1, slots_y1, y1_send, y1_recv),
    ]

    source = [a + b for a, b in zip(to_x(source_y), load[0])]
    for s in range(STEPS):
        exchange_x[s].start(line_x.message(source))
        if s == 0:
            line_x.weigh(share_x.arrived(), place_x)
        else:
            exchange_y[s - 1].close()
        inside = line_x.inside(source)
        base = [d * u - f + q for d, u, f, q in zip(twice_x, inside, source, load[s])]
        if s == 0:
            response_x = line_x.response(twice_x)
        source = respond(base, response_x, line_x.ends(exchange_x[s].arrived()))
        source_y = to_y(source)
        exchange_y[s].start(line_y.message(source_y))
        exchange_x[s].close()
        if s == 0:
            share_x.close()
            share_y.close()
            for sends, _, copy in halos:
                pl.when(sends)(copy.wait_send)
            line_y.weigh(share_y.arrived(), place_y)
        inside = line_y.inside(source_y)
        if s + 1 < STEPS:
            base = [d * u - f for d, u, f in zip(twice_y, inside, source_y)]
            if s == 0:
                response_y = line_y.response(twice_y)
            carried = respond(base, response_y, line_y.ends(exchange_y[s].arrived()))
            source = [a + b for a, b in zip(to_x(carried), load[s + 1])]
    drop = respond(inside, (line_y.near, line_y.far), line_y.ends(exchange_y[-1].arrived()))
    for k, part in enumerate(to_x(drop)):
        out_ref[pl.ds(k, SUB, stride=depth_x), :] = part

    exchange_y[-1].close()


def local(count_x, count_y, sag, warmth, store, load, flags):
    tile, pair = (SUB, 128), (2, 128)
    vmem = pl.BlockSpec(memory_space=pltpu.VMEM)

    def buffers(devices, shape):
        return [pltpu.VMEM(shape, jnp.float32), pltpu.VMEM((devices,) + shape, jnp.float32)]

    def semaphores():
        return [pltpu.SemaphoreType.DMA] * 2

    return pl.pallas_call(
        functools.partial(kernel, count_x, count_y),
        out_shape=pltpu.VMEM(sag.shape, jnp.float32),
        in_specs=[pl.BlockSpec(memory_space=pltpu.HBM)] * 5,
        out_specs=vmem,
        scratch_shapes=[
            *(pltpu.VMEM(x.shape, jnp.float32) for x in (sag, warmth, store, load)),
            pltpu.SMEM(flags.shape, jnp.int32),
            pltpu.SemaphoreType.DMA((5,)),
            pltpu.VMEM((sag.shape[1], sag.shape[0]), jnp.float32),
            pltpu.VMEM((2,) + tile, jnp.float32),
            pltpu.VMEM((2,) + tile, jnp.float32),
            *buffers(count_x, tile),
            *buffers(count_x, pair),
            *buffers(count_x, pair),
            *buffers(count_y, tile),
            *buffers(count_y, pair),
            *buffers(count_y, pair),
            pltpu.SemaphoreType.DMA((2,)),
            pltpu.SemaphoreType.DMA((2,)),
            *(semaphores() * 6),
        ],
        compiler_params=pltpu.CompilerParams(
            collective_id=0, has_side_effects=True, vmem_limit_bytes=16 * 2**20
        ),
    )(*(pltpu.with_memory_space_constraint(x, pltpu.HBM) for x in (sag, warmth, store, load, flags)))


def solution(mesh):
    return jax.shard_map(
        functools.partial(local, mesh.shape["gx"], mesh.shape["gy"]),
        mesh=mesh,
        in_specs=(P("gx", "gy"), P("gx", "gy"), P("gx", "gy"), P(None, "gx", "gy"), P("gx", "gy")),
        out_specs=P("gx", "gy"),
        check_vma=False,
    )
```

```python
import functools

import jax
import jax.numpy as jnp
from jax import lax
from jax.experimental import pallas as pl
from jax.experimental.pallas import tpu as pltpu
from jax.sharding import PartitionSpec as P

STEPS = 2
PITCH = 32
SUB = 8
SHORT = 1e20

xward_admittance = 1.0
yward_admittance = 0.5
warmth_scaling = 0.004
surrounding_warmth = 25.0
cushion_pieces = 1.0

MESH = pl.DeviceIdType.MESH


def roll(x, shift):
    return pltpu.roll(x, shift % x.shape[0], 0)


def sublanes(rows=SUB, lanes=128):
    return lax.broadcasted_iota(jnp.int32, (rows, lanes), 0)


def total(x):
    for step in (4, 2, 1):
        x = x + roll(x, step)
    return x


def tree(parts):
    while len(parts) > 1:
        parts = [functools.reduce(jnp.add, parts[k : k + 2]) for k in range(0, len(parts), 2)]
    return parts[0]


def both(pair):
    return jnp.broadcast_to(pair[0:1] + pair[1:2], (SUB, 128))


def wire(admittance, here, there):
    return admittance / (
        1.0 + warmth_scaling * (0.5 * (here + there) - surrounding_warmth)
    )


def pcr_factor(ground, link):
    rows = ground.shape[0]
    up = link
    down = jnp.where(sublanes(rows) == 0, 0.0, roll(link, 1))
    levels = []
    step = 1
    while step < rows:
        inverse = 1.0 / (ground + up + down)
        take_up = up * roll(inverse, -step)
        take_down = down * roll(inverse, step)
        levels.append((step, take_up, take_down))
        ground = ground + take_up * roll(ground, -step) + take_down * roll(ground, step)
        up, down = take_up * roll(up, -step), take_down * roll(down, step)
        step *= 2
    return levels, 1.0 / ground


def pcr_apply(factors, source):
    levels, inverse = factors
    for step, take_up, take_down in levels:
        source = source + take_up * roll(source, -step) + take_down * roll(source, step)
    return source * inverse


def chain_order(depth):
    order, step = [], 1
    while step < depth:
        order.append([(k, k - step, k + step) for k in range(step, depth, 2 * step)])
        step *= 2
    return order


def after(first, fill):
    return jnp.where(sublanes() == SUB - 1, fill, roll(first, -1))


class Line:
    def __init__(self, ground, link, warmth, admittance):
        depth = len(ground)
        self.depth = depth
        sub = sublanes()
        own = list(ground) + [jnp.zeros_like(ground[0])]
        right = list(link)
        right[-1] = jnp.where(sub == SUB - 1, SHORT, right[-1])
        self.admittance = admittance
        self.node = {}
        for level in chain_order(depth):
            for k, lo, hi in level:
                left_link, right_link = right[lo], right[k]
                inverse = 1.0 / (own[k] + left_link + right_link)
                to_lo, to_hi = left_link * inverse, right_link * inverse
                self.node[k] = (inverse, to_lo, to_hi)
                own[lo] = own[lo] + to_lo * own[k]
                own[hi] = own[hi] + to_hi * own[k]
                right[lo] = to_lo * right_link
        joined = right[0]
        held = own[0] + jnp.where(sub == 0, 0.0, roll(own[depth], 1))
        inner = sub > 0
        first_link = jnp.where(sub == 1, roll(joined, 1), 0.0)
        last_link = jnp.where(sub == SUB - 1, joined, 0.0)
        held = jnp.where(inner, held + first_link + last_link, 1.0)
        between = jnp.where(inner & (sub < SUB - 1), joined, 0.0)
        self.heads = pcr_factor(held, between)
        near = jnp.where(inner, pcr_apply(self.heads, first_link), 1.0)
        far = jnp.where(inner, pcr_apply(self.heads, last_link), 0.0)
        self.near = self.fill(near, after(near, 0.0))
        self.far = self.fill(far, after(far, 1.0))
        first = sub == 0
        bridge = jnp.where(first, joined * roll(far, -1), 0.0)
        near_ground, far_ground = self.condense(ground)
        rows = [total(near_ground), total(far_ground), roll(bridge, 2)]
        rows += [roll(warmth[0], 3), roll(warmth[-1], 5)]
        self.coefficients = jnp.zeros_like(ground[0])
        for r, row in enumerate(rows):
            self.coefficients = jnp.where(sub == r, row, self.coefficients)

    def fill(self, first, last, source=None):
        value = {0: first, self.depth: last}
        for level in reversed(chain_order(self.depth)):
            for k, lo, hi in level:
                inverse, to_lo, to_hi = self.node[k]
                out = to_lo * value[lo] + to_hi * value[hi]
                value[k] = out if source is None else source[k] * inverse + out
        return [value[k] for k in range(self.depth)]

    def condense(self, source):
        near = [a * b for a, b in zip(self.near, source)]
        far = [a * b for a, b in zip(self.far, source)]
        while len(near) > 1:
            near = [a + b for a, b in zip(near[::2], near[1::2])]
            far = [a + b for a, b in zip(far[::2], far[1::2])]
        return near[0], far[0]

    def message(self, source):
        near, far = self.condense(source)
        half = jnp.where(sublanes() < 4, near + roll(near, 4), far + roll(far, 4))
        half = half + roll(half, -2)
        half = half + roll(half, -1)
        return half[0:1], half[4:5]

    def inside(self, source):
        sub = sublanes()
        now = list(source) + [jnp.zeros_like(source[0])]
        for level in chain_order(self.depth):
            for k, lo, hi in level:
                _, to_lo, to_hi = self.node[k]
                now[lo] = now[lo] + to_lo * now[k]
                now[hi] = now[hi] + to_hi * now[k]
        head = jnp.where(sub == 0, 0.0, now[0] + roll(now[self.depth], 1))
        first = pcr_apply(self.heads, head)
        return self.fill(first, after(first, 0.0), now)

    def weigh(self, parts, place):
        devices = len(parts)
        rows = max(SUB, 2 * devices)
        at = sublanes(rows)
        ground = jnp.ones((rows, 128), jnp.float32)
        link = jnp.zeros((rows, 128), jnp.float32)
        for d, part in enumerate(parts):
            ground = jnp.where(at == 2 * d, part[0:1], ground)
            ground = jnp.where(at == 2 * d + 1, part[1:2], ground)
            link = jnp.where(at == 2 * d, part[2:3], link)
            if d + 1 < devices:
                between = wire(self.admittance, part[4:5], parts[d + 1][3:4])
                link = jnp.where(at == 2 * d + 1, between, link)
        factors = pcr_factor(ground, link)
        self.weights = []
        for kept in (2 * place, 2 * place + 1):
            row = pcr_apply(factors, jnp.where(at == kept, 1.0, 0.0))
            self.weights.append([row[2 * d : 2 * d + 2] for d in range(devices)])

    def ends(self, messages):
        return [
            both(tree([w * m for w, m in zip(weights, messages)])) for weights in self.weights
        ]

    def response(self, scale):
        return [c * p for c, p in zip(scale, self.near)], [c * p for c, p in zip(scale, self.far)]


def respond(base, response, ends):
    first, last = ends
    return [u + (p * first + q * last) for u, p, q in zip(base, *response)]


def carry(base, ends, ref):
    both_ends = jnp.concatenate(ends, 1)
    return tuple(
        row + jnp.dot(
            both_ends, ref[k],
            precision=lax.Precision.HIGHEST, preferred_element_type=jnp.float32,
        )[0:1]
        for k, row in enumerate(base)
    )


def partner(place, turn, devices):
    if devices & (devices - 1):
        return lax.rem(place + turn + 1, devices)
    flips, bit, other = devices - 1 - turn, 1, 0
    while bit < devices:
        here = lax.rem(lax.div(place, bit), 2)
        other = other + bit * (1 - here if flips & bit else here)
        bit *= 2
    return other


class Exchange:
    def __init__(self, axis, devices, mine, slots, send_sem, recv_sem):
        place = lax.axis_index(axis)
        self.copies = [
            pltpu.make_async_remote_copy(
                src_ref=mine,
                dst_ref=slots.at[place],
                send_sem=send_sem,
                recv_sem=recv_sem,
                device_id={axis: partner(place, turn, devices)},
                device_id_type=MESH,
            )
            for turn in range(devices - 1)
        ]
        self.place, self.devices, self.mine, self.slots = place, devices, mine, slots
        every = slots.at[pl.ds(0, devices - 1)]
        self.received = pltpu.make_async_copy(every, every, recv_sem)
        self.sent = pltpu.make_async_copy(every, every, send_sem)

    def start(self, value):
        if isinstance(value, tuple):
            for r, row in enumerate(value):
                self.mine[r : r + 1, :] = row
        else:
            self.mine[...] = value
        for copy in self.copies:
            copy.start()

    def arrived(self):
        self.received.wait()
        return [
            jnp.where(self.place == d, self.mine[...], self.slots[d]) for d in range(self.devices)
        ]

    def close(self):
        self.sent.wait()


def kernel(
    count_x, count_y,
    sag_hbm, warmth_hbm, store_hbm, load_hbm, flag_hbm,
    out_ref,
    sag_ref, warmth_ref, store_ref, load_ref, flag_ref, fetch_sem,
    turn_ref, to_y_ref, to_x_ref, halo_y, edge_y,
    mine_xc, slots_xc, mine_x0, slots_x0, mine_x1, slots_x1,
    mine_yc, slots_yc, mine_y0, slots_y0, mine_y1, slots_y1,
    halo_send, halo_recv,
    xc_send, xc_recv, x0_send, x0_recv, x1_send, x1_recv,
    yc_send, yc_recv, y0_send, y0_recv, y1_send, y1_recv,
):
    place_x = lax.axis_index("gx")
    place_y = lax.axis_index("gy")
    rows, cols = sag_ref.shape
    depth_x, depth_y = rows // SUB, cols // SUB
    sub = sublanes()
    lane = lax.broadcasted_iota(jnp.int32, (SUB, 128), 1)

    halo_y[...] = jnp.zeros_like(halo_y)
    barrier = pltpu.get_barrier_semaphore()
    for axis, place, devices in (("gy", place_y, count_y), ("gx", place_x, count_x)):
        for turn in range(devices - 1):
            pl.semaphore_signal(
                barrier, inc=1,
                device_id={axis: partner(place, turn, devices)}, device_id_type=MESH,
            )

    fetches = [
        pltpu.make_async_copy(src, dst, fetch_sem.at[k])
        for k, (src, dst) in enumerate([
            (warmth_hbm, warmth_ref), (sag_hbm, sag_ref), (store_hbm, store_ref),
            (flag_hbm, flag_ref), (load_hbm, load_ref),
        ])
    ]
    for fetch in fetches:
        fetch.start()

    def split(ref, depth):
        return [ref[pl.ds(k, SUB, stride=depth), :] for k in range(depth)]

    def to_y(parts):
        turn_ref[...] = jnp.concatenate(parts, 0).T
        return split(turn_ref, depth_y)

    def to_x(parts):
        for k, part in enumerate(parts):
            turn_ref[pl.ds(k, SUB, stride=depth_y), :] = part
        turned = turn_ref[...].T
        return [turned[SUB * k : SUB * k + SUB] for k in range(depth_x)]

    fetches[0].wait()
    fetches[1].wait()
    warmth_x = split(warmth_ref, depth_x)
    warmth_y = to_y(warmth_x)
    sag_y = to_y(split(sag_ref, depth_x))
    end_y = depth_y - 1
    edge_y[0] = jnp.where(sub == 0, warmth_y[0], roll(sag_y[0], 1))
    edge_y[1] = jnp.where(sub == 0, roll(warmth_y[end_y], 1), roll(sag_y[end_y], 2))

    pl.semaphore_wait(barrier, count_x - 1 + count_y - 1)

    halos = [
        (place_y > 0, place_y < count_y - 1, pltpu.make_async_remote_copy(
            src_ref=edge_y.at[0], dst_ref=halo_y.at[0],
            send_sem=halo_send.at[0], recv_sem=halo_recv.at[0],
            device_id={"gy": lax.rem(place_y + count_y - 1, count_y)}, device_id_type=MESH)),
        (place_y < count_y - 1, place_y > 0, pltpu.make_async_remote_copy(
            src_ref=edge_y.at[1], dst_ref=halo_y.at[1],
            send_sem=halo_send.at[1], recv_sem=halo_recv.at[1],
            device_id={"gy": lax.rem(place_y + 1, count_y)}, device_id_type=MESH)),
    ]
    for sends, _, copy in halos:
        pl.when(sends)(copy.start)

    fetches[2].wait()
    fetches[3].wait()
    store_x = split(store_ref, depth_x)
    store_y = to_y(store_x)
    cushion_x = jnp.zeros((SUB, 128), jnp.float32)
    cushion_y = jnp.zeros((SUB, 128), jnp.float32)
    for a in range(rows // PITCH):
        for b in range(cols // PITCH):
            flag = cushion_pieces * flag_ref[a, b].astype(jnp.float32)
            at_a, at_b = PITCH // depth_x * a, PITCH // depth_y * b
            cushion_x = jnp.where((sub == at_a) & (lane == PITCH * b), flag, cushion_x)
            cushion_y = jnp.where((sub == at_b) & (lane == at_a), flag, cushion_y)
    ground_x = [store_x[0] + cushion_x] + store_x[1:]
    ground_y = [store_y[0] + cushion_y] + store_y[1:]

    next_x = warmth_x[1:] + [roll(warmth_x[0], -1)]
    link_x = [wire(xward_admittance, a, b) for a, b in zip(warmth_x, next_x)]
    line_x = Line(ground_x, link_x, warmth_x, xward_admittance)
    share_x = Exchange("gx", count_x, mine_xc, slots_xc, xc_send, xc_recv)
    share_x.start(line_x.coefficients)

    next_y = warmth_y[1:] + [roll(warmth_y[0], -1)]
    link_y = [wire(yward_admittance, a, b) for a, b in zip(warmth_y, next_y)]
    line_y = Line(ground_y, link_y, warmth_y, yward_admittance)
    share_y = Exchange("gy", count_y, mine_yc, slots_yc, yc_send, yc_recv)
    share_y.start(line_y.coefficients)
    fetches[4].wait()
    load = [split(load_ref.at[s], depth_x) for s in range(STEPS)]
    twice_x = [2.0 * c for c in store_x]
    twice_y = [2.0 * c for c in store_y]
    flow = [g * (a - b) for g, a, b in zip(link_y[:-1], sag_y[:-1], sag_y[1:])]
    kept = [c * v for c, v in zip(store_y, sag_y)]
    kept[0] = kept[0] - cushion_y * sag_y[0]
    inner = [k - (o - i) for k, o, i in zip(kept[1:-1], flow[1:], flow[:-1])]

    for _, receives, copy in halos:
        pl.when(receives)(copy.wait_recv)

    last_y = (sub == SUB - 1) & (place_y == count_y - 1)
    first_y = (sub == 0) & (place_y == 0)
    next_warmth = after(warmth_y[0], halo_y[0, 0:1])
    next_sag = after(sag_y[0], halo_y[0, 1:2])
    outflow = wire(yward_admittance, warmth_y[-1], next_warmth) * (sag_y[-1] - next_sag)
    outflow = jnp.where(last_y, 0.0, outflow)
    inflow = wire(yward_admittance, halo_y[1, 0:1], warmth_y[0]) * (halo_y[1, 1:2] - sag_y[0])
    inflow = jnp.where(first_y, 0.0, inflow)
    inflow = jnp.where(sub == 0, inflow, roll(outflow, 1))
    source_y = [kept[0] - (flow[0] - inflow), *inner, kept[-1] - (outflow - flow[-1])]

    exchange_x = [
        Exchange("gx", count_x, mine_x0, slots_x0, x0_send, x0_recv),
        Exchange("gx", count_x, mine_x1, slots_x1, x1_send, x1_recv),
    ]
    exchange_y = [
        Exchange("gy", count_y, mine_y0, slots_y0, y0_send, y0_recv),
        Exchange("gy", count_y, mine_y1, slots_y1, y1_send, y1_recv),
    ]

    source = [a + b for a, b in zip(to_x(source_y), load[0])]
    exchange_x[0].start(line_x.message(source))
    line_x.weigh(share_x.arrived(), place_x)
    for s in range(STEPS):
        if s > 0:
            exchange_y[s - 1].close()
        inside = line_x.inside(source)
        base = [d * u - f + q for d, u, f, q in zip(twice_x, inside, source, load[s])]
        if s == 0:
            response_x = line_x.response(twice_x)
            for half, response in enumerate(response_x):
                for k, part in enumerate(to_y(response)):
                    at = pl.ds(128 * half + k, SUB, stride=depth_y)
                    to_y_ref[0, at, :] = line_y.near[k] * part
                    to_y_ref[1, at, :] = line_y.far[k] * part
        message = line_y.message(to_y(base))
        ends = line_x.ends(exchange_x[s].arrived())
        exchange_y[s].start(carry(message, ends, to_y_ref))
        source_y = to_y(respond(base, response_x, ends))
        exchange_x[s].close()
        if s == 0:
            share_x.close()
            share_y.close()
            for sends, _, copy in halos:
                pl.when(sends)(copy.wait_send)
            line_y.weigh(share_y.arrived(), place_y)
        inside = line_y.inside(source_y)
        if s + 1 < STEPS:
            base = [d * u - f for d, u, f in zip(twice_y, inside, source_y)]
            if s == 0:
                response_y = line_y.response(twice_y)
                for half, response in enumerate(response_y):
                    for k, part in enumerate(to_x(response)):
                        at = pl.ds(128 * half + SUB * k, SUB)
                        to_x_ref[0, at, :] = line_x.near[k] * part
                        to_x_ref[1, at, :] = line_x.far[k] * part
            message = line_x.message([a + b for a, b in zip(to_x(base), load[s + 1])])
            ends = line_y.ends(exchange_y[s].arrived())
            exchange_x[s + 1].start(carry(message, ends, to_x_ref))
            carried = respond(base, response_y, ends)
            source = [a + b for a, b in zip(to_x(carried), load[s + 1])]
    drop = respond(inside, (line_y.near, line_y.far), line_y.ends(exchange_y[-1].arrived()))
    for k, part in enumerate(to_x(drop)):
        out_ref[pl.ds(k, SUB, stride=depth_x), :] = part

    exchange_y[-1].close()


def local(count_x, count_y, sag, warmth, store, load, flags):
    tile, pair = (SUB, 128), (2, 128)
    vmem = pl.BlockSpec(memory_space=pltpu.VMEM)

    def buffers(devices, shape):
        return [pltpu.VMEM(shape, jnp.float32), pltpu.VMEM((devices,) + shape, jnp.float32)]

    def semaphores():
        return [pltpu.SemaphoreType.DMA] * 2

    return pl.pallas_call(
        functools.partial(kernel, count_x, count_y),
        out_shape=pltpu.VMEM(sag.shape, jnp.float32),
        in_specs=[pl.BlockSpec(memory_space=pltpu.HBM)] * 5,
        out_specs=vmem,
        scratch_shapes=[
            *(pltpu.VMEM(x.shape, jnp.float32) for x in (sag, warmth, store, load)),
            pltpu.SMEM(flags.shape, jnp.int32),
            pltpu.SemaphoreType.DMA((5,)),
            pltpu.VMEM((sag.shape[1], sag.shape[0]), jnp.float32),
            pltpu.VMEM((2, 256, 128), jnp.float32),
            pltpu.VMEM((2, 256, 128), jnp.float32),
            pltpu.VMEM((2,) + tile, jnp.float32),
            pltpu.VMEM((2,) + tile, jnp.float32),
            *buffers(count_x, tile),
            *buffers(count_x, pair),
            *buffers(count_x, pair),
            *buffers(count_y, tile),
            *buffers(count_y, pair),
            *buffers(count_y, pair),
            pltpu.SemaphoreType.DMA((2,)),
            pltpu.SemaphoreType.DMA((2,)),
            *(semaphores() * 6),
        ],
        compiler_params=pltpu.CompilerParams(
            collective_id=0, has_side_effects=True, vmem_limit_bytes=16 * 2**20
        ),
    )(*(pltpu.with_memory_space_constraint(x, pltpu.HBM) for x in (sag, warmth, store, load, flags)))


def solution(mesh):
    return jax.shard_map(
        functools.partial(local, mesh.shape["gx"], mesh.shape["gy"]),
        mesh=mesh,
        in_specs=(P("gx", "gy"), P("gx", "gy"), P("gx", "gy"), P(None, "gx", "gy"), P("gx", "gy")),
        out_specs=P("gx", "gy"),
        check_vma=False,
    )
```

```python
import functools

import jax
import jax.numpy as jnp
from jax import lax
from jax.experimental import pallas as pl
from jax.experimental.pallas import tpu as pltpu
from jax.sharding import PartitionSpec as P

STEPS = 2
PITCH = 32
SUB = 8
SHORT = 1e20

xward_admittance = 1.0
yward_admittance = 0.5
warmth_scaling = 0.004
surrounding_warmth = 25.0
cushion_pieces = 1.0

MESH = pl.DeviceIdType.MESH


def roll(x, shift):
    return pltpu.roll(x, shift % x.shape[0], 0)


def sublanes(rows=SUB, lanes=128):
    return lax.broadcasted_iota(jnp.int32, (rows, lanes), 0)


def total(x):
    for step in (4, 2, 1):
        x = x + roll(x, step)
    return x


def tree(parts):
    while len(parts) > 1:
        parts = [functools.reduce(jnp.add, parts[k : k + 2]) for k in range(0, len(parts), 2)]
    return parts[0]


def both(pair):
    return jnp.broadcast_to(pair[0:1] + pair[1:2], (SUB, 128))


def wire(admittance, here, there):
    return admittance / (
        1.0 + warmth_scaling * (0.5 * (here + there) - surrounding_warmth)
    )


def pcr_factor(ground, link):
    rows = ground.shape[0]
    up = link
    down = jnp.where(sublanes(rows) == 0, 0.0, roll(link, 1))
    levels = []
    step = 1
    while step < rows:
        inverse = 1.0 / (ground + up + down)
        take_up = up * roll(inverse, -step)
        take_down = down * roll(inverse, step)
        levels.append((step, take_up, take_down))
        ground = ground + take_up * roll(ground, -step) + take_down * roll(ground, step)
        up, down = take_up * roll(up, -step), take_down * roll(down, step)
        step *= 2
    return levels, 1.0 / ground


def pcr_apply(factors, source):
    levels, inverse = factors
    for step, take_up, take_down in levels:
        source = source + take_up * roll(source, -step) + take_down * roll(source, step)
    return source * inverse


def chain_order(depth):
    order, step = [], 1
    while step < depth:
        order.append([(k, k - step, k + step) for k in range(step, depth, 2 * step)])
        step *= 2
    return order


def after(first, fill):
    return jnp.where(sublanes() == SUB - 1, fill, roll(first, -1))


class Line:
    def __init__(self, ground, link, warmth, admittance):
        depth = len(ground)
        self.depth = depth
        sub = sublanes()
        own = list(ground) + [jnp.zeros_like(ground[0])]
        right = list(link)
        right[-1] = jnp.where(sub == SUB - 1, SHORT, right[-1])
        self.admittance = admittance
        self.node = {}
        for level in chain_order(depth):
            for k, lo, hi in level:
                left_link, right_link = right[lo], right[k]
                inverse = 1.0 / (own[k] + left_link + right_link)
                to_lo, to_hi = left_link * inverse, right_link * inverse
                self.node[k] = (inverse, to_lo, to_hi)
                own[lo] = own[lo] + to_lo * own[k]
                own[hi] = own[hi] + to_hi * own[k]
                right[lo] = to_lo * right_link
        joined = right[0]
        held = own[0] + jnp.where(sub == 0, 0.0, roll(own[depth], 1))
        inner = sub > 0
        first_link = jnp.where(sub == 1, roll(joined, 1), 0.0)
        last_link = jnp.where(sub == SUB - 1, joined, 0.0)
        held = jnp.where(inner, held + first_link + last_link, 1.0)
        between = jnp.where(inner & (sub < SUB - 1), joined, 0.0)
        self.heads = pcr_factor(held, between)
        near = jnp.where(inner, pcr_apply(self.heads, first_link), 1.0)
        far = jnp.where(inner, pcr_apply(self.heads, last_link), 0.0)
        self.near = self.fill(near, after(near, 0.0))
        self.far = self.fill(far, after(far, 1.0))
        first = sub == 0
        bridge = jnp.where(first, joined * roll(far, -1), 0.0)
        near_ground, far_ground = self.condense(ground)
        rows = [total(near_ground), total(far_ground), roll(bridge, 2)]
        rows += [roll(warmth[0], 3), roll(warmth[-1], 5)]
        self.coefficients = jnp.zeros_like(ground[0])
        for r, row in enumerate(rows):
            self.coefficients = jnp.where(sub == r, row, self.coefficients)

    def fill(self, first, last, source=None):
        value = {0: first, self.depth: last}
        for level in reversed(chain_order(self.depth)):
            for k, lo, hi in level:
                inverse, to_lo, to_hi = self.node[k]
                out = to_lo * value[lo] + to_hi * value[hi]
                value[k] = out if source is None else source[k] * inverse + out
        return [value[k] for k in range(self.depth)]

    def condense(self, source):
        near = [a * b for a, b in zip(self.near, source)]
        far = [a * b for a, b in zip(self.far, source)]
        while len(near) > 1:
            near = [a + b for a, b in zip(near[::2], near[1::2])]
            far = [a + b for a, b in zip(far[::2], far[1::2])]
        return near[0], far[0]

    def message(self, source):
        near, far = self.condense(source)
        half = jnp.where(sublanes() < 4, near + roll(near, 4), far + roll(far, 4))
        half = half + roll(half, -2)
        half = half + roll(half, -1)
        return half[0:1], half[4:5]

    def inside(self, source):
        sub = sublanes()
        now = list(source) + [jnp.zeros_like(source[0])]
        for level in chain_order(self.depth):
            for k, lo, hi in level:
                _, to_lo, to_hi = self.node[k]
                now[lo] = now[lo] + to_lo * now[k]
                now[hi] = now[hi] + to_hi * now[k]
        head = jnp.where(sub == 0, 0.0, now[0] + roll(now[self.depth], 1))
        first = pcr_apply(self.heads, head)
        return self.fill(first, after(first, 0.0), now)

    def weigh(self, parts, place):
        devices = len(parts)
        rows = max(SUB, 2 * devices)
        at = sublanes(rows)
        ground = jnp.ones((rows, 128), jnp.float32)
        link = jnp.zeros((rows, 128), jnp.float32)
        for d, part in enumerate(parts):
            ground = jnp.where(at == 2 * d, part[0:1], ground)
            ground = jnp.where(at == 2 * d + 1, part[1:2], ground)
            link = jnp.where(at == 2 * d, part[2:3], link)
            if d + 1 < devices:
                between = wire(self.admittance, part[4:5], parts[d + 1][3:4])
                link = jnp.where(at == 2 * d + 1, between, link)
        factors = pcr_factor(ground, link)
        self.weights = []
        for kept in (2 * place, 2 * place + 1):
            row = pcr_apply(factors, jnp.where(at == kept, 1.0, 0.0))
            self.weights.append([row[2 * d : 2 * d + 2] for d in range(devices)])

    def ends(self, messages):
        return [
            both(tree([w * m for w, m in zip(weights, messages)])) for weights in self.weights
        ]

    def response(self, scale):
        return [c * p for c, p in zip(scale, self.near)], [c * p for c, p in zip(scale, self.far)]


def respond(base, response, ends):
    first, last = ends
    return [u + (p * first + q * last) for u, p, q in zip(base, *response)]


def partner(place, turn, devices):
    if devices & (devices - 1):
        return lax.rem(place + turn + 1, devices)
    flips, bit, other = devices - 1 - turn, 1, 0
    while bit < devices:
        here = lax.rem(lax.div(place, bit), 2)
        other = other + bit * (1 - here if flips & bit else here)
        bit *= 2
    return other


class Exchange:
    def __init__(self, axis, devices, mine, slots, send_sem, recv_sem):
        place = lax.axis_index(axis)
        self.copies = [
            pltpu.make_async_remote_copy(
                src_ref=mine,
                dst_ref=slots.at[place],
                send_sem=send_sem,
                recv_sem=recv_sem,
                device_id={axis: partner(place, turn, devices)},
                device_id_type=MESH,
            )
            for turn in range(devices - 1)
        ]
        self.place, self.devices, self.mine, self.slots = place, devices, mine, slots
        every = slots.at[pl.ds(0, devices - 1)]
        self.received = pltpu.make_async_copy(every, every, recv_sem)
        self.sent = pltpu.make_async_copy(every, every, send_sem)

    def start(self, value):
        if isinstance(value, tuple):
            for r, row in enumerate(value):
                self.mine[r : r + 1, :] = row
        else:
            self.mine[...] = value
        for copy in self.copies:
            copy.start()

    def arrived(self):
        self.received.wait()
        return [
            jnp.where(self.place == d, self.mine[...], self.slots[d]) for d in range(self.devices)
        ]

    def close(self):
        self.sent.wait()


def kernel(
    count_x, count_y,
    sag_hbm, warmth_hbm, store_hbm, load_hbm, flag_hbm,
    out_ref,
    sag_ref, warmth_ref, store_ref, load_ref, flag_ref, fetch_sem,
    turn_ref, halo_y, edge_y,
    mine_xc, slots_xc, mine_x0, slots_x0, mine_x1, slots_x1,
    mine_yc, slots_yc, mine_y0, slots_y0, mine_y1, slots_y1,
    halo_send, halo_recv,
    xc_send, xc_recv, x0_send, x0_recv, x1_send, x1_recv,
    yc_send, yc_recv, y0_send, y0_recv, y1_send, y1_recv,
):
    place_x = lax.axis_index("gx")
    place_y = lax.axis_index("gy")
    rows, cols = sag_ref.shape
    depth_x, depth_y = rows // SUB, cols // SUB
    sub = sublanes()
    lane = lax.broadcasted_iota(jnp.int32, (SUB, 128), 1)

    halo_y[...] = jnp.zeros_like(halo_y)
    barrier = pltpu.get_barrier_semaphore()
    for axis, place, devices in (("gy", place_y, count_y), ("gx", place_x, count_x)):
        for turn in range(devices - 1):
            pl.semaphore_signal(
                barrier, inc=1,
                device_id={axis: partner(place, turn, devices)}, device_id_type=MESH,
            )

    fetches = [
        pltpu.make_async_copy(src, dst, fetch_sem.at[k])
        for k, (src, dst) in enumerate([
            (warmth_hbm, warmth_ref), (sag_hbm, sag_ref), (store_hbm, store_ref),
            (flag_hbm, flag_ref), (load_hbm, load_ref),
        ])
    ]
    for fetch in fetches:
        fetch.start()

    def split(ref, depth):
        return [ref[pl.ds(k, SUB, stride=depth), :] for k in range(depth)]

    def to_y(parts):
        turn_ref[...] = jnp.concatenate(parts, 0).T
        return split(turn_ref, depth_y)

    def to_x(parts):
        for k, part in enumerate(parts):
            turn_ref[pl.ds(k, SUB, stride=depth_y), :] = part
        turned = turn_ref[...].T
        return [turned[SUB * k : SUB * k + SUB] for k in range(depth_x)]

    fetches[0].wait()
    fetches[1].wait()
    warmth_x = split(warmth_ref, depth_x)
    warmth_y = to_y(warmth_x)
    sag_y = to_y(split(sag_ref, depth_x))
    end_y = depth_y - 1
    edge_y[0] = jnp.where(sub == 0, warmth_y[0], roll(sag_y[0], 1))
    edge_y[1] = jnp.where(sub == 0, roll(warmth_y[end_y], 1), roll(sag_y[end_y], 2))

    pl.semaphore_wait(barrier, count_x - 1 + count_y - 1)

    halos = [
        (place_y > 0, place_y < count_y - 1, pltpu.make_async_remote_copy(
            src_ref=edge_y.at[0], dst_ref=halo_y.at[0],
            send_sem=halo_send.at[0], recv_sem=halo_recv.at[0],
            device_id={"gy": lax.rem(place_y + count_y - 1, count_y)}, device_id_type=MESH)),
        (place_y < count_y - 1, place_y > 0, pltpu.make_async_remote_copy(
            src_ref=edge_y.at[1], dst_ref=halo_y.at[1],
            send_sem=halo_send.at[1], recv_sem=halo_recv.at[1],
            device_id={"gy": lax.rem(place_y + 1, count_y)}, device_id_type=MESH)),
    ]
    for sends, _, copy in halos:
        pl.when(sends)(copy.start)

    fetches[2].wait()
    fetches[3].wait()
    store_x = split(store_ref, depth_x)
    store_y = to_y(store_x)
    cushion_x = jnp.zeros((SUB, 128), jnp.float32)
    cushion_y = jnp.zeros((SUB, 128), jnp.float32)
    for a in range(rows // PITCH):
        for b in range(cols // PITCH):
            flag = cushion_pieces * flag_ref[a, b].astype(jnp.float32)
            at_a, at_b = PITCH // depth_x * a, PITCH // depth_y * b
            cushion_x = jnp.where((sub == at_a) & (lane == PITCH * b), flag, cushion_x)
            cushion_y = jnp.where((sub == at_b) & (lane == at_a), flag, cushion_y)
    ground_x = [store_x[0] + cushion_x] + store_x[1:]
    ground_y = [store_y[0] + cushion_y] + store_y[1:]

    next_x = warmth_x[1:] + [roll(warmth_x[0], -1)]
    link_x = [wire(xward_admittance, a, b) for a, b in zip(warmth_x, next_x)]
    line_x = Line(ground_x, link_x, warmth_x, xward_admittance)
    share_x = Exchange("gx", count_x, mine_xc, slots_xc, xc_send, xc_recv)
    share_x.start(line_x.coefficients)

    next_y = warmth_y[1:] + [roll(warmth_y[0], -1)]
    link_y = [wire(yward_admittance, a, b) for a, b in zip(warmth_y, next_y)]
    line_y = Line(ground_y, link_y, warmth_y, yward_admittance)
    share_y = Exchange("gy", count_y, mine_yc, slots_yc, yc_send, yc_recv)
    fetches[4].wait()
    load = [split(load_ref.at[s], depth_x) for s in range(STEPS)]
    twice_x = [2.0 * c for c in store_x]
    twice_y = [2.0 * c for c in store_y]
    flow = [g * (a - b) for g, a, b in zip(link_y[:-1], sag_y[:-1], sag_y[1:])]
    kept = [c * v for c, v in zip(store_y, sag_y)]
    kept[0] = kept[0] - cushion_y * sag_y[0]
    inner = [k - (o - i) for k, o, i in zip(kept[1:-1], flow[1:], flow[:-1])]

    for _, receives, copy in halos:
        pl.when(receives)(copy.wait_recv)

    last_y = (sub == SUB - 1) & (place_y == count_y - 1)
    first_y = (sub == 0) & (place_y == 0)
    next_warmth = after(warmth_y[0], halo_y[0, 0:1])
    next_sag = after(sag_y[0], halo_y[0, 1:2])
    outflow = wire(yward_admittance, warmth_y[-1], next_warmth) * (sag_y[-1] - next_sag)
    outflow = jnp.where(last_y, 0.0, outflow)
    inflow = wire(yward_admittance, halo_y[1, 0:1], warmth_y[0]) * (halo_y[1, 1:2] - sag_y[0])
    inflow = jnp.where(first_y, 0.0, inflow)
    inflow = jnp.where(sub == 0, inflow, roll(outflow, 1))
    source_y = [kept[0] - (flow[0] - inflow), *inner, kept[-1] - (outflow - flow[-1])]

    exchange_x = [
        Exchange("gx", count_x, mine_x0, slots_x0, x0_send, x0_recv),
        Exchange("gx", count_x, mine_x1, slots_x1, x1_send, x1_recv),
    ]
    exchange_y = [
        Exchange("gy", count_y, mine_y0, slots_y0, y0_send, y0_recv),
        Exchange("gy", count_y, mine_y1, slots_y1, y1_send, y1_recv),
    ]

    source = [a + b for a, b in zip(to_x(source_y), load[0])]
    for s in range(STEPS):
        exchange_x[s].start(line_x.message(source))
        if s == 0:
            share_y.start(line_y.coefficients)
            line_x.weigh(share_x.arrived(), place_x)
        else:
            exchange_y[s - 1].close()
        inside = line_x.inside(source)
        base = [d * u - f + q for d, u, f, q in zip(twice_x, inside, source, load[s])]
        if s == 0:
            response_x = line_x.response(twice_x)
        source = respond(base, response_x, line_x.ends(exchange_x[s].arrived()))
        source_y = to_y(source)
        exchange_y[s].start(line_y.message(source_y))
        exchange_x[s].close()
        if s == 0:
            share_x.close()
            share_y.close()
            for sends, _, copy in halos:
                pl.when(sends)(copy.wait_send)
            line_y.weigh(share_y.arrived(), place_y)
        inside = line_y.inside(source_y)
        if s + 1 < STEPS:
            base = [d * u - f for d, u, f in zip(twice_y, inside, source_y)]
            if s == 0:
                response_y = line_y.response(twice_y)
            carried = respond(base, response_y, line_y.ends(exchange_y[s].arrived()))
            source = [a + b for a, b in zip(to_x(carried), load[s + 1])]
    exchange_y[-1].close()
    drop = respond(inside, (line_y.near, line_y.far), line_y.ends(exchange_y[-1].arrived()))
    for k, part in enumerate(to_x(drop)):
        out_ref[pl.ds(k, SUB, stride=depth_x), :] = part


def local(count_x, count_y, sag, warmth, store, load, flags):
    tile, pair = (SUB, 128), (2, 128)
    vmem = pl.BlockSpec(memory_space=pltpu.VMEM)

    def buffers(devices, shape):
        return [pltpu.VMEM(shape, jnp.float32), pltpu.VMEM((devices,) + shape, jnp.float32)]

    def semaphores():
        return [pltpu.SemaphoreType.DMA] * 2

    return pl.pallas_call(
        functools.partial(kernel, count_x, count_y),
        out_shape=pltpu.VMEM(sag.shape, jnp.float32),
        in_specs=[pl.BlockSpec(memory_space=pltpu.HBM)] * 5,
        out_specs=vmem,
        scratch_shapes=[
            *(pltpu.VMEM(x.shape, jnp.float32) for x in (sag, warmth, store, load)),
            pltpu.SMEM(flags.shape, jnp.int32),
            pltpu.SemaphoreType.DMA((5,)),
            pltpu.VMEM((sag.shape[1], sag.shape[0]), jnp.float32),
            pltpu.VMEM((2,) + tile, jnp.float32),
            pltpu.VMEM((2,) + tile, jnp.float32),
            *buffers(count_x, tile),
            *buffers(count_x, pair),
            *buffers(count_x, pair),
            *buffers(count_y, tile),
            *buffers(count_y, pair),
            *buffers(count_y, pair),
            pltpu.SemaphoreType.DMA((2,)),
            pltpu.SemaphoreType.DMA((2,)),
            *(semaphores() * 6),
        ],
        compiler_params=pltpu.CompilerParams(
            collective_id=0, has_side_effects=True, vmem_limit_bytes=16 * 2**20
        ),
    )(*(pltpu.with_memory_space_constraint(x, pltpu.HBM) for x in (sag, warmth, store, load, flags)))


def solution(mesh):
    return jax.shard_map(
        functools.partial(local, mesh.shape["gx"], mesh.shape["gy"]),
        mesh=mesh,
        in_specs=(P("gx", "gy"), P("gx", "gy"), P("gx", "gy"), P(None, "gx", "gy"), P("gx", "gy")),
        out_specs=P("gx", "gy"),
        check_vma=False,
    )
```
